128 devices in a mesh: dom: 64 (over y, x, z), rep: 2 (over core).
Axes of the slice: x: 4, y: 4, z: 4, core: 2. Of those that a mesh axis runs over, the one named last changes fastest.
Arguments:
- features: bfloat16 [131072, 256], P('dom', 'rep'), may hold values from -6 to 6
- cotangent: bfloat16 [131072, 256], P('dom', 'rep'), may hold values from -6 to 6
- self_weight: bfloat16 [256, 256], P('rep'), may hold values from -0.375 to 0.375
- neighbor_weight: bfloat16 [256, 256], P('rep'), may hold values from -0.375 to 0.375
- local_neighbors: int32 [131072, 8], P('dom'), may hold values from 0 to 2047
- hub_rows: int32 [2048], P('dom'), may hold values from 0 to 2047
- hub_neighbors: int32 [131072, 4], P('dom'), may hold values from 0 to 2047
- boundary_rows: int32 [16384], P('dom'), may hold values from 0 to 2047
- send_lists: int32 [64, 64, 128], P('dom'), may hold values from 0 to 255
- received_counts: int32 [64, 64], P('dom'), may hold values from 1 to 128, as said below
- halo_neighbors: int32 [131072, 4], P('dom'), may hold values from 0 to 8064, as said below
Outputs:
- output: bfloat16 [131072, 256], P('dom', 'rep')
- grad_features: bfloat16 [131072, 256], P('dom', 'rep')
- grad_self: float32 [256, 256], P('rep')
- grad_neighbor: float32 [256, 256], P('rep')
The draws below stay inside these ranges and needn't reach their ends.
Inputs may be any that keep to these rules, and one draw needn't show every extreme that they name: Every row of received_counts has one entry equal to 128 and one entry equal to 1; partition 0 receives 128 live slots from every partition except one. An entry of halo_neighbors for a node of partition d is below the sum of row d of received_counts: it counts the live slots that d receives, ordered by sending partition and then by slot.
All inputs are finite; a program needn't handle non-finite values.
Results may differ from the reference program's by a relative error of at most 0.005.
Values may be sent and summed in bfloat16 or wider, within the bound.
A program may use at most 128 MiB of HBM per device.

```python
import math
import jax
import jax.numpy as jnp
import numpy as np

D = 256
V_DEV = 2048
K_LOC = 8
K_HALO = 4
K_HUB = 4
C = 128
B_DEV = 256
H_DEV = 32
NODES = 131072
HUBS = 2048
N_DOM = 64


def live_counts(key):
    domains = NODES // V_DEV
    keys = jax.random.split(jax.random.fold_in(key, 11), 4)
    ceiling = jax.random.randint(keys[0], (domains, 1), C // 2, C + 1)
    counts = jax.random.randint(keys[1], (domains, domains), ceiling // 2, ceiling + 1)
    full_column = jax.random.randint(keys[2], (domains,), 0, domains)
    single_column = (full_column + jax.random.randint(keys[3], (domains,), 1, domains)) % domains
    columns = jnp.arange(domains)[None, :]
    rows = jnp.arange(domains)[:, None]
    counts = jnp.where(rows == 0, C, counts)
    counts = jnp.where(columns == full_column[:, None], C, counts)
    counts = jnp.where(columns == single_column[:, None], 1, counts)
    return counts.astype(jnp.int32)


def draw_received_counts(key, part):
    return live_counts(key)


def draw_halo_neighbors(key, part):
    counts = live_counts(key)
    row_totals = jnp.sum(counts, axis=1)
    totals = jnp.repeat(row_totals, V_DEV)
    entries = jax.random.randint(jax.random.fold_in(key, 23), (NODES, K_HALO), 0, totals[:, None])
    entries = entries.at[0, 0].set(row_totals[0] - 1)
    entries = entries.at[1, 0].set(0)
    return entries.astype(jnp.int32)


def place_ends(values, stream_key, least, high):
    dims = values.shape
    spot = [jax.random.randint(jax.random.fold_in(stream_key, axis), (), 0, dims[axis]) for axis in range(len(dims))]
    values = values.at[tuple(spot)].set(least)
    longest = dims.index(max(dims))
    spot[longest] = (spot[longest] + 1) % dims[longest]
    return values.at[tuple(spot)].set(high)


def block_scale(rng, extent, cuts, smallest, high):
    loudness = 1.0
    for axis_at, shards_of in cuts:
        draws = jax.random.uniform(jax.random.fold_in(jax.random.fold_in(rng, 6), axis_at), (shards_of,), jnp.float32, smallest / len(cuts), high / len(cuts))
        loudness = loudness * jnp.repeat(jnp.exp(draws), extent[axis_at] // shards_of).reshape((-1,) + (1,) * (len(extent) - 1 - axis_at))
    return loudness


def cumulative_ranks(number_of, slope):
    loads = [(1 << 20) // math.isqrt(standing ** slope) + 1 for standing in range(1, number_of + 1)]
    width = 1 + sum(loads) // (1 << 30)
    return np.cumsum(np.array([max(1, weight // width) for weight in loads]))


def skewed_ids(own_key, shape, amount, lean):
    grid = cumulative_ranks(amount, lean)
    lot = jax.random.randint(jax.random.fold_in(own_key, 1), shape, 0, int(grid[amount - 1]))
    standing = jnp.searchsorted(jnp.asarray(grid, jnp.int32), lot, side="right")
    return jax.random.permutation(jax.random.fold_in(own_key, 2), amount)[standing].astype(jnp.int32)


def noise(own_key, shape, width, most, cuts=(), kind=jnp.bfloat16):
    array = jax.random.normal(own_key, shape, jnp.float32) * width
    if len(cuts) > 0:
        array = block_scale(own_key, shape, cuts, -0.22, 0.18) * array
    return jnp.clip(array, min=-most, max=most).astype(kind)


def setup_inputs(seed: int = 0) -> dict:
    splits = jax.random.split(jax.random.key(seed), 12)
    features = noise(splits[0], (NODES, D), 1.0, 6.0, ((0, 64), (1, 2)))
    cotangent = noise(splits[1], (NODES, D), 1.0, 6.0, ((0, 64), (1, 2)))
    self_weight = noise(splits[2], (D, D), D ** -0.5, 0.375, ((0, 2),))
    neighbor_weight = noise(splits[3], (D, D), D ** -0.5, 0.375, ((0, 2),))
    local_neighbors = place_ends(jax.random.randint(splits[4], (NODES, K_LOC), 0, V_DEV), jax.random.fold_in(splits[4], 1), 0, V_DEV - 1).astype(jnp.int32)
    hub_rows = place_ends(jax.random.randint(splits[5], (HUBS,), 0, V_DEV), jax.random.fold_in(splits[5], 1), 0, V_DEV - 1).astype(jnp.int32)
    hub_neighbors = place_ends(skewed_ids(splits[6], (NODES, K_HUB), HUBS, 1), jax.random.fold_in(splits[6], 3), 0, HUBS - 1).astype(jnp.int32)
    boundary_rows = place_ends(jax.random.randint(splits[7], (N_DOM * B_DEV,), 0, V_DEV), jax.random.fold_in(splits[7], 1), 0, V_DEV - 1).astype(jnp.int32)
    send_lists = place_ends(jax.random.randint(splits[8], (N_DOM, N_DOM, C), 0, B_DEV), jax.random.fold_in(splits[8], 1), 0, B_DEV - 1).astype(jnp.int32)
    received_counts = draw_received_counts(jax.random.fold_in(splits[11], 71), 0)
    halo_neighbors = draw_halo_neighbors(jax.random.fold_in(splits[11], 71), 0)
    return dict(features=features, cotangent=cotangent, self_weight=self_weight, neighbor_weight=neighbor_weight, local_neighbors=local_neighbors, hub_rows=hub_rows, hub_neighbors=hub_neighbors, boundary_rows=boundary_rows, send_lists=send_lists, received_counts=received_counts, halo_neighbors=halo_neighbors)


def halo_global_rows(boundary_rows, send_lists, received_counts, halo_neighbors):
    boundary_global = (jnp.arange(N_DOM * B_DEV, dtype=jnp.int32) // B_DEV) * V_DEV + boundary_rows
    lists_by_receiver = jnp.transpose(send_lists, (1, 0, 2))
    sender_base = (jnp.arange(N_DOM, dtype=jnp.int32) * B_DEV)[None, :, None]
    slot_global = boundary_global[(sender_base + lists_by_receiver).reshape(-1)].reshape(N_DOM, N_DOM * C)
    entries = halo_neighbors.reshape(N_DOM, V_DEV, K_HALO)
    count_ends = jnp.cumsum(received_counts, axis=1)
    passed_ends = count_ends[:, None, None, :] <= entries[..., None]
    sender = jnp.minimum(jnp.sum(passed_ends.astype(jnp.int32), -1), N_DOM - 1)
    before = jnp.sum(jnp.where(passed_ends, received_counts[:, None, None, :], 0), -1)
    position = jnp.clip(entries - before, 0, C - 1)
    flat_slot = (sender * C + position).reshape(N_DOM, V_DEV * K_HALO).astype(jnp.int32)
    return jnp.take_along_axis(slot_global, flat_slot, axis=1).reshape(NODES, K_HALO)


def reference(features, cotangent, self_weight, neighbor_weight, local_neighbors, hub_rows, hub_neighbors, boundary_rows, send_lists, received_counts, halo_neighbors):
    node_base = (jnp.arange(NODES, dtype=jnp.int32) // V_DEV) * V_DEV
    local_global = node_base[:, None] + local_neighbors
    hub_global = (jnp.arange(HUBS, dtype=jnp.int32) // H_DEV) * V_DEV + hub_rows
    hub_neighbor_rows = hub_global[hub_neighbors]
    halo_rows = halo_global_rows(boundary_rows, send_lists, received_counts, halo_neighbors)
    neighbors = jnp.concatenate([local_global, halo_rows, hub_neighbor_rows], axis=1).astype(jnp.int32)
    fan_total = neighbors.shape[1]
    summed = jnp.zeros((NODES, D), jnp.float32)
    for column in range(fan_total):
        summed = summed + features[neighbors[:, column]].astype(jnp.float32)
    aggregate = (summed / fan_total).astype(jnp.bfloat16)
    pre_act = jnp.dot(features, self_weight, preferred_element_type=jnp.float32) + jnp.dot(aggregate, neighbor_weight, preferred_element_type=jnp.float32)
    output = jax.nn.silu(pre_act).astype(jnp.bfloat16)
    sigmoid_value = jax.nn.sigmoid(pre_act)
    derivative = sigmoid_value * (1.0 + pre_act * (1.0 - sigmoid_value))
    out_grad = (cotangent.astype(jnp.float32) * derivative).astype(jnp.bfloat16)
    norm_factor = float(NODES) ** -0.5
    grad_self = jnp.dot(features.T, out_grad, preferred_element_type=jnp.float32) * norm_factor
    grad_neighbor = jnp.dot(aggregate.T, out_grad, preferred_element_type=jnp.float32) * norm_factor
    back_agg = jnp.dot(out_grad, neighbor_weight.T, preferred_element_type=jnp.float32) / fan_total
    gradient = jnp.dot(out_grad, self_weight.T, preferred_element_type=jnp.float32)
    for column in range(fan_total):
        gradient = gradient.at[neighbors[:, column]].add(back_agg)
    return output, gradient.astype(jnp.bfloat16), grad_self, grad_neighbor
```

```python
import functools

import jax
import jax.numpy as jnp
from jax import lax
from jax.experimental import pallas as pl
from jax.experimental.pallas import tpu as pltpu
from jax.sharding import PartitionSpec as P

MESH = pl.DeviceIdType.MESH
VMEM_SPEC = pl.BlockSpec(memory_space=pltpu.VMEM)
STRIDE = {"y": 16, "x": 4, "z": 1}
CHAINS = (("y", "x", "z"), ("z", "y", "x"), ("x", "z", "y"))
UNIT = 96
BIG = 58 * 2**20


def place():
    dom = lax.axis_index("dom")
    rep = lax.axis_index("rep")
    at = {"y": dom // 16, "x": (dom // 4) % 4, "z": dom % 4}
    return dom, rep, at


def shifted(dom, at, axis, delta):
    there = (at[axis] + delta) % 4
    return dom + (there - at[axis]) * STRIDE[axis]


def greet(dom, rep, at):
    barrier = pltpu.get_barrier_semaphore()
    for axis in "yxz":
        for delta in (1, 2, 3):
            pl.semaphore_signal(
                barrier, inc=1, device_id=(shifted(dom, at, axis, delta), rep), device_id_type=MESH
            )
    pl.semaphore_signal(barrier, inc=1, device_id=(dom, 1 - rep), device_id_type=MESH)
    pl.semaphore_wait(barrier, 10)


class Copies:
    def __init__(self, send, recv):
        self.send, self.recv, self.used, self.open = send, recv, 0, []

    def take(self):
        self.used += 1
        return self.used - 1

    def start(self, number, src, dst, device):
        copy = pltpu.make_async_remote_copy(
            src_ref=src,
            dst_ref=dst,
            send_sem=self.send.at[number],
            recv_sem=self.recv.at[number],
            device_id=device,
            device_id_type=MESH,
        )
        copy.start()
        self.open.append(copy)

    def arrived(self, number, dst, device):
        pltpu.make_async_remote_copy(
            src_ref=dst,
            dst_ref=dst,
            send_sem=self.send.at[number],
            recv_sem=self.recv.at[number],
            device_id=device,
            device_id_type=MESH,
        ).wait_recv()

    def close(self):
        for copy in self.open:
            copy.wait_send()
        self.open = []


def zhalf(ref, chain, half, lead=()):
    two = pl.ds(2 * half, 2)
    if chain == 0:
        return ref.at[lead + (slice(None), slice(None), two)]
    if chain == 1:
        return ref.at[lead + (two,)]
    return ref.at[lead + (slice(None), two)]


N_GATHER = 3 * 12 + 3 * 3 + 9 + 3


def gather_kernel(
    u0, u1, u2, lists, feat, cot, wts, t0, t1, t2, l3, featx, cotx, wtsx, g0, g1, g2, l1, l2, send, recv, local
):
    dom, rep, at = place()
    other = (dom, 1 - rep)
    units, bufs, tables = (u0, u1, u2), (g0, g1, g2), (t0, t1, t2)
    io = Copies(send, recv)
    greet(dom, rep, at)

    mine = []
    for chain in range(3):
        o, m, i = (at[a] for a in CHAINS[chain])
        copy = pltpu.make_async_copy(units[chain], bufs[chain].at[o, m, i], local.at[chain])
        copy.start()
        mine.append(copy)
    own = pltpu.make_async_copy(lists.at[at["y"]], l1.at[at["y"]], local.at[3])
    own.start()

    def block(chain, step, delta):
        o, m, i = (at[a] for a in CHAINS[chain])
        if step == 0:
            return bufs[chain].at[o, m, (i + delta) % 4]
        if step == 1:
            return bufs[chain].at[o, (m + delta) % 4]
        return bufs[chain].at[(o + delta) % 4]

    def half(chain, step, delta, which):
        o, m, i = (at[a] for a in CHAINS[chain])
        if step == 0:
            return bufs[chain].at[o, m, (i + delta) % 4, pl.ds(which * (UNIT // 2), UNIT // 2)]
        if step == 1:
            return bufs[chain].at[o, (m + delta) % 4, pl.ds(which * 2, 2)]
        return bufs[chain].at[(o + delta) % 4, pl.ds(which * 2, 2)]

    list_steps = (
        ("y", lambda j: lists.at[j], lambda j: l1.at[j]),
        ("x", lambda j: l1.at[:, j], lambda j: l2.at[j]),
        ("z", lambda j: l2.at[:, :, j], lambda j: l3.at[j]),
    )
    list_ids = [[io.take() for _ in range(3)] for _ in range(3)]

    def send_lists(step):
        axis, src, dst = list_steps[step]
        for delta in (1, 2, 3):
            there = (at[axis] + delta) % 4
            io.start(
                list_ids[step][delta - 1],
                src(there),
                dst(at[axis]),
                (shifted(dom, at, axis, delta), rep),
            )

    def take_lists(step):
        axis, _, dst = list_steps[step]
        for delta in (1, 2, 3):
            io.arrived(list_ids[step][delta - 1], dst((at[axis] - delta) % 4), other)

    send_lists(0)
    theirs = pl.ds((1 - rep) * 1024, 1024)
    pair_ids = [io.take() for _ in range(3)]
    pairs = ((feat.at[theirs], featx), (cot.at[theirs], cotx), (wts, wtsx))

    swap_ids = [io.take() for _ in range(3)]
    for step in range(3):
        ids = {}
        for chain in range(3):
            axis = CHAINS[chain][2 - step]
            up, down = (shifted(dom, at, axis, 1), rep), (shifted(dom, at, axis, 3), rep)
            if step == 0:
                mine[chain].wait()
            ids[chain] = [io.take() for _ in range(4)]
            io.start(ids[chain][0], block(chain, step, 0), block(chain, step, 0), up)
            io.start(ids[chain][1], block(chain, step, 0), block(chain, step, 0), down)
        if step == 0:
            for number, (src, dst) in zip(pair_ids, pairs):
                io.start(number, src, dst, other)
            own.wait()
        take_lists(step)
        if step < 2:
            axis, src, dst = list_steps[step + 1]
            copy = pltpu.make_async_copy(src(at[axis]), dst(at[axis]), local.at[3])
            copy.start()
            send_lists(step + 1)
            copy.wait()
        for chain in range(3):
            axis = CHAINS[chain][2 - step]
            up, down = (shifted(dom, at, axis, 1), rep), (shifted(dom, at, axis, 3), rep)
            io.arrived(ids[chain][0], block(chain, step, 3), down)
            io.start(ids[chain][2], half(chain, step, 3, 0), half(chain, step, 3, 0), up)
            io.arrived(ids[chain][1], block(chain, step, 1), up)
            io.start(ids[chain][3], half(chain, step, 1, 1), half(chain, step, 1, 1), down)
        for chain in range(3):
            axis = CHAINS[chain][2 - step]
            up, down = (shifted(dom, at, axis, 1), rep), (shifted(dom, at, axis, 3), rep)
            io.arrived(ids[chain][2], half(chain, step, 2, 0), down)
            io.arrived(ids[chain][3], half(chain, step, 2, 1), up)
    keep = []
    for chain in range(3):
        io.start(swap_ids[chain], zhalf(bufs[chain], chain, 1 - rep), tables[chain].at[rep], other)
        copy = pltpu.make_async_copy(
            zhalf(bufs[chain], chain, rep), tables[chain].at[rep], local.at[chain]
        )
        copy.start()
        keep.append(copy)
    for chain in range(3):
        keep[chain].wait()
        io.arrived(swap_ids[chain], tables[chain].at[1 - rep], other)
    for number, (_, dst) in zip(pair_ids, pairs):
        io.arrived(number, dst, other)
    io.close()


TSHAPES = ((2, 4, 4, 2, UNIT, 128), (2, 2, 4, 4, UNIT, 128), (2, 4, 2, 4, UNIT, 128))


def gather_call(units, lists, feat, cot, wts):
    bf = jnp.bfloat16
    return pl.pallas_call(
        gather_kernel,
        out_shape=[jax.ShapeDtypeStruct(s, bf) for s in TSHAPES]
        + [
            jax.ShapeDtypeStruct((4, 4, 4, 1, 128), jnp.int32),
            jax.ShapeDtypeStruct((1024, 128), bf),
            jax.ShapeDtypeStruct((1024, 128), bf),
            jax.ShapeDtypeStruct((256, 256), bf),
        ],
        in_specs=[VMEM_SPEC] * 7,
        out_specs=[VMEM_SPEC] * 7,
        scratch_shapes=[pltpu.VMEM((4, 4, 4, UNIT, 128), bf)] * 3
        + [pltpu.VMEM((4, 4, 4, 1, 128), jnp.int32)] * 2
        + [
            pltpu.SemaphoreType.DMA((N_GATHER,)),
            pltpu.SemaphoreType.DMA((N_GATHER,)),
            pltpu.SemaphoreType.DMA((4,)),
        ],
        compiler_params=pltpu.CompilerParams(
            collective_id=0, has_side_effects=True, vmem_limit_bytes=BIG
        ),
        name="gather_rows",
    )(*units, lists, feat, cot, wts)


def one_hot(picks, counts, rows, base):
    nodes = picks[0].shape[1]
    row = lax.broadcasted_iota(jnp.int16, (rows, nodes), 0)
    table = jnp.zeros((rows, nodes), jnp.bfloat16)
    for pick, count in zip(picks, counts):
        here = jnp.broadcast_to(pick - base, (rows, nodes)).astype(jnp.int16)
        table = jnp.where(
            here == row, jnp.broadcast_to(count.astype(jnp.bfloat16), (rows, nodes)), table
        )
    return table


def ones_at(pick, rows, base=0):
    row = lax.broadcasted_iota(jnp.int32, (rows, pick.shape[1]), 0)
    return jnp.where(pick - base == row, 1.0, 0.0).astype(jnp.bfloat16)


def dot(a, b, over_a=1, over_b=0):
    return lax.dot_general(
        a, b, (((over_a,), (over_b,)), ((), ())), preferred_element_type=jnp.float32
    )


def side_by_side(rep, own, other, axis):
    first = jnp.where(rep == 0, own, other)
    second = jnp.where(rep == 0, other, own)
    return jnp.concatenate([first, second], axis=axis)


def prepare_kernel(counts, raw, rows, feat, picks, mult, units):
    rep = lax.axis_index("rep")
    halo = raw[8:12]
    end = jnp.int32(0)
    sender = jnp.zeros_like(halo)
    before = jnp.zeros_like(halo)
    for p in range(64):
        end = end + counts[0, p]
        passed = halo >= end
        sender = sender + jnp.where(passed, 1, 0)
        before = before + jnp.where(passed, counts[0, p], 0)
    sender = jnp.minimum(sender, 63)
    slot = jnp.clip(halo - before, 0, 127)

    def in_half(p, within, size):
        number = (p >> 2) * 2 + (p & 1)
        return jnp.where(((p & 3) >> 1) == rep, number * size + within, -1)

    hub = raw[12:16]
    local = raw[0:8] - rep * 1024
    local = jnp.where((local >= 0) & (local < 1024), local, -1)
    groups = (local, in_half(sender, slot, 128), in_half(hub >> 5, hub & 31, 32))
    start = 0
    for group in groups:
        size = group.shape[0]
        picks[start : start + size] = group
        for a in range(size):
            total = jnp.zeros((1, group.shape[1]), jnp.float32)
            for b in range(size):
                total = total + jnp.where(group[a : a + 1] == group[b : b + 1], 1.0, 0.0)
            mult[start + a : start + a + 1] = total
        start += size
    chooser = ones_at(rows[...], 2048)
    units[...] = dot(chooser, feat[...], 0, 0).astype(jnp.bfloat16)


def plain(kernel, out_shape, args, name, smem=(), grid=None, scratch=(), in_specs=None, out_specs=None):
    if in_specs is None:
        in_specs = [
            pl.BlockSpec(memory_space=pltpu.SMEM) if n in smem else VMEM_SPEC for n in range(len(args))
        ]
    if out_specs is None:
        out_specs = [VMEM_SPEC] * len(out_shape)
    return pl.pallas_call(
        kernel,
        out_shape=out_shape,
        in_specs=in_specs,
        out_specs=out_specs,
        grid=() if grid is None else grid,
        scratch_shapes=list(scratch),
        compiler_params=pltpu.CompilerParams(vmem_limit_bytes=BIG),
        name=name,
    )(*args)


def chain_index(number):
    y, x, z = number // 8, (number // 2) % 4, number % 2
    return number, z * 16 + y * 4 + x, x * 8 + z * 4 + y


def forward_kernel(picks, mult, t0, t1, t2, lists, feat, featx, out, table):
    rep = lax.axis_index("rep")

    @pl.when(pl.program_id(0) == 0)
    def build():
        for number in range(32):
            i0, i1, i2 = chain_index(number)
            wide = [
                jnp.concatenate([t[0, i], t[1, i]], axis=1) for t, i in ((t0, i0), (t1, i1), (t2, i2))
            ]
            rows = jnp.concatenate([wide[0], wide[1], wide[2][:64]], axis=0)
            y, x, z = number // 8, (number // 2) % 4, number % 2
            chosen = lists[pl.ds(rep * 32 + z * 16 + x * 4 + y, 1)]
            slots = dot(ones_at(chosen, 256), rows, 0, 0)
            table[1024 + number * 128 : 1024 + number * 128 + 128] = slots.astype(jnp.bfloat16)
            table[5120 + number * 32 : 5120 + number * 32 + 32] = wide[2][64:]
        own = feat[pl.ds(pl.multiple_of(rep * 1024, 1024), 1024)]
        table[0:1024] = side_by_side(rep, own, featx[...], 1)

    total = jnp.zeros((picks.shape[1], 256), jnp.float32)
    for first, some, begin, end in ((0, 8, 0, 1024), (8, 4, 1024, 5120), (12, 4, 5120, 6144)):
        chosen = [picks[k : k + 1] for k in range(first, first + some)]
        counts = [mult[k : k + 1] for k in range(first, first + some)]
        for base in range(begin, end, 512):
            total = total + dot(
                one_hot(chosen, counts, 512, base - begin), table[base : base + 512], 0, 0
            )
    out[...] = total


def forward_call(picks, mult, tables, lists, feat, featx):
    full = lambda a: pl.BlockSpec(a.shape, lambda i: (0,) * a.ndim)
    tile = pl.BlockSpec((16, 512), lambda i: (0, i))
    args = [picks, mult, *tables, lists, feat, featx]
    return plain(
        forward_kernel,
        [jax.ShapeDtypeStruct((2048, 256), jnp.float32)],
        args,
        "gather_sum",
        grid=(4,),
        scratch=[pltpu.VMEM((6144, 256), jnp.bfloat16)],
        in_specs=[tile, tile] + [full(a) for a in args[2:]],
        out_specs=[pl.BlockSpec((512, 256), lambda i: (i, 0))],
    )[0]


def middle_kernel(total, totalx, feat, featx, cot, cotx, wts, wtsx, send, agg_own, out_own):
    rep = lax.axis_index("rep")
    mine = pl.ds(pl.multiple_of(rep * 1024, 1024), 1024)
    selfw = side_by_side(rep, wts[0:128], wtsx[0:128], 0)
    nbrw = side_by_side(rep, wts[128:256], wtsx[128:256], 0)
    for step in range(4):
        rows = pl.ds(pl.multiple_of(rep * 1024, 1024) + step * 256, 256)
        part = slice(step * 256, step * 256 + 256)
        features = side_by_side(rep, feat[rows], featx[part], 1)
        cotangent = side_by_side(rep, cot[rows], cotx[part], 1)
        aggregate = ((total[rows] + totalx[part]) * (1.0 / 16.0)).astype(jnp.bfloat16)
        pre_act = dot(features, selfw) + dot(aggregate, nbrw)
        sigmoid = 1.0 / (1.0 + jnp.exp(-pre_act))
        output = (pre_act * sigmoid).astype(jnp.bfloat16)
        slope = sigmoid * (1.0 + pre_act * (1.0 - sigmoid))
        grad = (cotangent.astype(jnp.float32) * slope).astype(jnp.bfloat16)
        send[part, 0:256] = grad
        send[part, 256:384] = jnp.where(rep == 0, aggregate[:, 128:], aggregate[:, :128])
        send[part, 384:512] = jnp.where(rep == 0, output[:, 128:], output[:, :128])
        agg_own[part] = jnp.where(rep == 0, aggregate[:, :128], aggregate[:, 128:])
        out_own[part] = jnp.where(rep == 0, output[:, :128], output[:, 128:])


def backward_kernel(
    picks, mult, lists, feat, sent, got, agg_own, out_own, u0, u1, u2, local, terms, output, grad
):
    rep = lax.axis_index("rep")
    mine = pl.ds(pl.multiple_of(rep * 1024, 1024), 1024)
    theirs = pl.ds(pl.multiple_of((1 - rep) * 1024, 1024), 1024)
    step = pl.program_id(0)

    @pl.when(step == 0)
    def once():
        grad[mine] = sent[:, 0:256]
        grad[theirs] = got[:, 0:256]
        output[mine] = out_own[...]
        output[theirs] = got[:, 384:512]
        selft = dot(feat[...], grad[...], 0, 0)
        nbrt = dot(agg_own[...], sent[:, 0:256], 0, 0) + dot(got[:, 256:384], got[:, 0:256], 0, 0)
        for n, term in enumerate((selft, nbrt)):
            terms[2 * n] = term[:, :128]
            terms[2 * n + 1] = term[:, 128:]

    total = jnp.zeros((768, 256), jnp.float32)
    for begin in range(0, 2048, 256):
        cols = slice(begin, begin + 256)
        parts = []
        for first, some, rows in ((0, 8, 128), (8, 4, 512), (12, 4, 128)):
            chosen = [picks[k : k + 1, cols] for k in range(first, first + some)]
            counts = [mult[k : k + 1, cols] for k in range(first, first + some)]
            parts.append(one_hot(chosen, counts, rows, step * rows))
        total = total + dot(jnp.concatenate(parts, axis=0), grad[cols])
    local[pl.ds(pl.multiple_of(step * 128, 128), 128)] = total[0:128]
    slots = total[128:640].astype(jnp.bfloat16)
    hubs = total[640:768].astype(jnp.bfloat16)
    for k in range(4):
        number = step * 4 + k
        y, x, z = number // 8, (number // 2) % 4, number % 2
        chosen = lists[pl.ds(rep * 32 + z * 16 + x * 4 + y, 1)]
        rows = dot(ones_at(chosen, 256), slots[k * 128 : k * 128 + 128]).astype(jnp.bfloat16)
        i0, i1, i2 = chain_index(number)
        for h in range(2):
            cols = slice(h * 128, h * 128 + 128)
            u0[h, i0] = rows[0:96, cols]
            u1[h, i1] = rows[96:192, cols]
            u2[h, i2, 0:64] = rows[192:256, cols]
            u2[h, i2, 64:96] = hubs[k * 32 : k * 32 + 32, cols]


def backward_call(*args):
    full = lambda a: pl.BlockSpec(a.shape, lambda i: (0,) * len(a.shape))
    shapes = [jax.ShapeDtypeStruct((2, 32, UNIT, 128), jnp.bfloat16)] * 3 + [
        jax.ShapeDtypeStruct((1024, 256), jnp.float32),
        jax.ShapeDtypeStruct((4, 128, 128), jnp.float32),
        jax.ShapeDtypeStruct((2048, 128), jnp.bfloat16),
    ]
    return plain(
        backward_kernel,
        shapes,
        args,
        "scatter_sum",
        grid=(8,),
        scratch=[pltpu.VMEM((2048, 256), jnp.bfloat16)],
        in_specs=[full(a) for a in args],
        out_specs=[full(s) for s in shapes],
    )


N_SCATTER = 3 + 3 * 18 + 18 + 3


def scatter_kernel(u0, u1, u2, terms, r0, r1, r2, sums, *rest):
    bufs = rest[0:3]
    nexts = (rest[3:6], rest[6:9])
    recvs = [rest[9 + 4 * n : 13 + 4 * n] for n in range(9)]
    w1, w2, wb, wc, w3 = rest[45:50]
    send, recv, localsem = rest[50:53]
    dom, rep, at = place()
    other = (dom, 1 - rep)
    units, results = (u0, u1, u2), (r0, r1, r2)
    io = Copies(send, recv)
    greet(dom, rep, at)

    swap_ids = [io.take() for _ in range(3)]
    keep = []
    for chain in range(3):
        io.start(swap_ids[chain], units[chain].at[1 - rep], zhalf(bufs[chain], chain, rep), other)
        copy = pltpu.make_async_copy(
            units[chain].at[rep], zhalf(bufs[chain], chain, rep), localsem.at[chain]
        )
        copy.start()
        keep.append(copy)

    def peers(axis):
        return [
            (delta, (at[axis] + delta) % 4, (shifted(dom, at, axis, delta), rep)) for delta in (1, 2, 3)
        ]

    def reduce_along(axis, src, landing):
        ids = [io.take() for _ in range(3)]
        for delta, there, device in peers(axis):
            io.start(ids[delta - 1], src.at[there], landing.at[delta - 1], device)
        for delta in (1, 2, 3):
            io.arrived(ids[delta - 1], landing.at[delta - 1], other)

    reduce_along("y", terms, w1)
    wb[...] = terms[at["y"]] + w1[0] + w1[1] + w1[2]
    reduce_along("x", wb, w2)
    wc[...] = wb[at["x"]] + w2[0] + w2[1] + w2[2]
    reduce_along("z", wc, w3)
    sums[at["y"], at["x"], at["z"]] = wc[at["z"]] + w3[0] + w3[1] + w3[2]

    def hand_out(axis, ref, start):
        if start:
            ids = [io.take() for _ in range(3)]
            for delta, _, device in peers(axis):
                io.start(ids[delta - 1], ref(at[axis]), ref(at[axis]), device)
            return ids

    def hand_in(axis, ref, ids):
        for delta in (1, 2, 3):
            io.arrived(ids[delta - 1], ref((at[axis] - delta) % 4), other)

    gives = (
        ("z", lambda j: sums.at[at["y"], at["x"], j]),
        ("x", lambda j: sums.at[at["y"], j]),
        ("y", lambda j: sums.at[j]),
    )

    for chain in range(3):
        keep[chain].wait()
        io.arrived(swap_ids[chain], zhalf(bufs[chain], chain, 1 - rep), other)

    now = list(bufs)
    for step in range(3):
        ids = [[io.take() for _ in range(6)] for _ in range(3)]
        lows = pl.ds(0, UNIT // 2) if step == 2 else pl.ds(0, 2)
        highs = pl.ds(UNIT // 2, UNIT // 2) if step == 2 else pl.ds(2, 2)
        loops = (8, 2, 1)[step]

        def ends(chain):
            axis = CHAINS[chain][step]
            i = at[axis]
            up, down = (shifted(dom, at, axis, 1), rep), (shifted(dom, at, axis, 3), rep)
            return i, (i + 1) % 4, (i + 2) % 4, (i + 3) % 4, up, down

        def unit(ref, lead, low, k):
            if step == 0:
                return ref.at[lead + (low * 2 + k // 4, k % 4)]
            if step == 1:
                return ref.at[lead + (low * 2 + k,)]
            return ref.at[lead + (pl.ds(low * (UNIT // 2), UNIT // 2),)]

        for chain in range(3):
            i, above, far, below, up, down = ends(chain)
            data, (from_low, from_high, whole_low, whole_high) = now[chain], recvs[3 * step + chain]
            n = ids[chain]
            io.start(n[0], data.at[far, lows], from_low, up)
            io.start(n[1], data.at[far, highs], from_high, down)
            io.start(n[2], data.at[above, highs], whole_low.at[highs], up)
            io.start(n[3], data.at[below, lows], whole_high.at[lows], down)
        axis, ref = gives[step]
        given = hand_out(axis, ref, True)
        hand_in(axis, ref, given)
        for chain in range(3):
            i, above, far, below, up, down = ends(chain)
            data, (from_low, from_high, whole_low, whole_high) = now[chain], recvs[3 * step + chain]
            n = ids[chain]
            for number, landing, lead, low, target, device in (
                (0, from_low, above, 0, whole_low, up),
                (1, from_high, below, 1, whole_high, down),
            ):
                io.arrived(n[number], landing, other)

                def add(k, carry, landing=landing, lead=lead, low=low):
                    spot = unit(data, (lead,), low, k)
                    came = unit(landing, (), 0, k)
                    spot[...] = (
                        spot[...].astype(jnp.float32) + came[...].astype(jnp.float32)
                    ).astype(jnp.bfloat16)
                    return carry

                lax.fori_loop(0, loops, add, 0)
                part = lows if low == 0 else highs
                io.start(n[4 + number], data.at[lead, part], target.at[part], device)
        for chain in range(3):
            i, above, far, below, up, down = ends(chain)
            data, (from_low, from_high, whole_low, whole_high) = now[chain], recvs[3 * step + chain]
            n = ids[chain]
            io.arrived(n[2], whole_low.at[highs], other)
            io.arrived(n[4], whole_low.at[lows], other)
            io.arrived(n[3], whole_high.at[lows], other)
            io.arrived(n[5], whole_high.at[highs], other)
            target = nexts[step][chain] if step < 2 else results[chain].at[rep]

            def total(k, carry):
                low, rest_k = (k // loops, k % loops)
                value = (
                    unit(data, (i,), low, rest_k)[...].astype(jnp.float32)
                    + unit(whole_low, (), low, rest_k)[...].astype(jnp.float32)
                    + unit(whole_high, (), low, rest_k)[...].astype(jnp.float32)
                )
                spot = unit(target, (), low, rest_k)
                spot[...] = value.astype(target.dtype)
                return carry

            if step == 2:
                target[...] = (
                    data[i].astype(jnp.float32)
                    + whole_low[...].astype(jnp.float32)
                    + whole_high[...].astype(jnp.float32)
                )
            else:
                lax.fori_loop(0, 2 * loops, total, 0)
        if step < 2:
            now = list(nexts[step])
    last = [io.take() for _ in range(3)]
    for chain in range(3):
        io.start(last[chain], results[chain].at[rep], results[chain].at[rep], other)
    for chain in range(3):
        io.arrived(last[chain], results[chain].at[1 - rep], other)
    io.close()


def scatter_call(units, terms):
    bf, f32 = jnp.bfloat16, jnp.float32
    recvs = []
    for lead in ((4, 4), (4,), ()):
        whole = lead + (UNIT, 128)
        half = (whole[0] // 2,) + whole[1:]
        for _ in range(3):
            recvs += [pltpu.VMEM(s, bf) for s in (half, half, whole, whole)]
    return pl.pallas_call(
        scatter_kernel,
        out_shape=[jax.ShapeDtypeStruct((2, UNIT, 128), f32)] * 3
        + [jax.ShapeDtypeStruct((4, 4, 4, 8, 128), f32)],
        in_specs=[VMEM_SPEC] * 4,
        out_specs=[VMEM_SPEC] * 4,
        scratch_shapes=[pltpu.VMEM((4, 4, 4, UNIT, 128), bf)] * 3
        + [pltpu.VMEM((4, 4, UNIT, 128), bf)] * 3
        + [pltpu.VMEM((4, UNIT, 128), bf)] * 3
        + recvs
        + [
            pltpu.VMEM((3, 4, 4, 8, 128), f32),
            pltpu.VMEM((3, 4, 8, 128), f32),
            pltpu.VMEM((4, 4, 8, 128), f32),
            pltpu.VMEM((4, 8, 128), f32),
            pltpu.VMEM((3, 8, 128), f32),
            pltpu.SemaphoreType.DMA((N_SCATTER,)),
            pltpu.SemaphoreType.DMA((N_SCATTER,)),
            pltpu.SemaphoreType.DMA((3,)),
        ],
        compiler_params=pltpu.CompilerParams(
            collective_id=1, has_side_effects=True, vmem_limit_bytes=BIG
        ),
        name="scatter_rows",
    )(*units, terms)


def final_kernel(rows, r0, r1, r2, local, sent, wts, wtsx, keep, give):
    rep = lax.axis_index("rep")
    selfw = side_by_side(rep, wts[0:128], wtsx[0:128], 0)
    nbrw = side_by_side(rep, wts[128:256], wtsx[128:256], 0)
    totals = jnp.concatenate(
        [jnp.concatenate([r[0], r[1]], axis=1) for r in (r0, r1, r2)], axis=0
    )
    high = totals.astype(jnp.bfloat16)
    low = (totals - high.astype(jnp.float32)).astype(jnp.bfloat16)
    for step in range(4):
        part = slice(step * 256, step * 256 + 256)
        chooser = ones_at(rows[...], 256, rep * 1024 + step * 256)
        sums = local[part] + dot(chooser, high) + dot(chooser, low)
        sums = (sums * (1.0 / 16.0)).astype(jnp.bfloat16)
        value = dot(sent[part, 0:256], selfw, 1, 1) + dot(sums, nbrw, 1, 1)
        value = value.astype(jnp.bfloat16)
        keep[part] = jnp.where(rep == 0, value[:, :128], value[:, 128:])
        give[part] = jnp.where(rep == 0, value[:, 128:], value[:, :128])


PAIR = ((0, 1), (1, 0))


def per_device(
    features,
    cotangent,
    self_weight,
    neighbor_weight,
    local_neighbors,
    hub_rows,
    hub_neighbors,
    boundary_rows,
    send_lists,
    received_counts,
    halo_neighbors,
):
    bf, f32 = jnp.bfloat16, jnp.float32
    rep = lax.axis_index("rep")
    raw = jnp.concatenate([local_neighbors, halo_neighbors, hub_neighbors], axis=1).T
    rows = jnp.concatenate([boundary_rows, hub_rows])[None]
    picks, mult, units = plain(
        prepare_kernel,
        [
            jax.ShapeDtypeStruct((16, 2048), jnp.int32),
            jax.ShapeDtypeStruct((16, 2048), f32),
            jax.ShapeDtypeStruct((288, 128), bf),
        ],
        [received_counts, raw, rows, features],
        "prepare",
        smem=(0,),
    )
    weights = jnp.concatenate([self_weight, neighbor_weight], axis=0)
    *tables, lists, featx, cotx, wtsx = gather_call(
        [units[UNIT * c : UNIT * c + UNIT] for c in range(3)],
        send_lists.reshape(4, 4, 4, 1, 128),
        features,
        cotangent,
        weights,
    )
    tables = [t.reshape(2, 32, UNIT, 128) for t in tables]
    lists = lists.reshape(64, 128)
    total = forward_call(picks, mult, tables, lists, features, featx)
    theirs = lax.dynamic_slice_in_dim(total, (1 - rep) * 1024, 1024, 0)
    totalx = lax.ppermute(theirs, "rep", PAIR)
    sent, agg_own, out_own = plain(
        middle_kernel,
        [
            jax.ShapeDtypeStruct((1024, 512), bf),
            jax.ShapeDtypeStruct((1024, 128), bf),
            jax.ShapeDtypeStruct((1024, 128), bf),
        ],
        [total, totalx, features, featx, cotangent, cotx, weights, wtsx],
        "middle",
    )
    got = lax.ppermute(sent, "rep", PAIR)
    u0, u1, u2, local, terms, output = backward_call(
        picks, mult, lists, features, sent, got, agg_own, out_own
    )
    r0, r1, r2, sums = scatter_call(
        [u.reshape(s) for u, s in zip((u0, u1, u2), TSHAPES)], terms.reshape(4, 4, 4, 8, 128)
    )
    keep, give = plain(
        final_kernel,
        [jax.ShapeDtypeStruct((1024, 128), bf)] * 2,
        [rows, r0, r1, r2, local, sent, weights, wtsx],
        "final",
    )
    came = lax.ppermute(give, "rep", PAIR)
    gradient = side_by_side(rep, keep, came, 0)
    sums = sums.reshape(2, 2, 128, 128) * (131072.0**-0.5)
    sums = jnp.concatenate([sums[:, 0], sums[:, 1]], axis=2)
    return output, gradient, sums[0], sums[1]


def solution(mesh):
    return jax.shard_map(
        per_device,
        mesh=mesh,
        in_specs=(
            P("dom", "rep"),
            P("dom", "rep"),
            P("rep", None),
            P("rep", None),
            P("dom", None),
            P("dom"),
            P("dom", None),
            P("dom"),
            P("dom", None, None),
            P("dom", None),
            P("dom", None),
        ),
        out_specs=(P("dom", "rep"), P("dom", "rep"), P("rep", None), P("rep", None)),
        check_vma=False,
    )
```

```python
import functools

import jax
import jax.numpy as jnp
from jax import lax
from jax.experimental import pallas as pl
from jax.experimental.pallas import tpu as pltpu
from jax.sharding import PartitionSpec as P

MESH = pl.DeviceIdType.MESH
VMEM_SPEC = pl.BlockSpec(memory_space=pltpu.VMEM)
STRIDE = {"y": 16, "x": 4, "z": 1}
CHAINS = (("y", "x", "z"), ("z", "y", "x"), ("x", "z", "y"))
UNIT = 96
BIG = 58 * 2**20


def place():
    dom = lax.axis_index("dom")
    rep = lax.axis_index("rep")
    at = {"y": dom // 16, "x": (dom // 4) % 4, "z": dom % 4}
    return dom, rep, at


def shifted(dom, at, axis, delta):
    there = (at[axis] + delta) % 4
    return dom + (there - at[axis]) * STRIDE[axis]


def signal_all(dom, rep, at):
    barrier = pltpu.get_barrier_semaphore()
    for axis in "yxz":
        for delta in (1, 2, 3):
            pl.semaphore_signal(
                barrier, inc=1, device_id=(shifted(dom, at, axis, delta), rep), device_id_type=MESH
            )
    pl.semaphore_signal(barrier, inc=1, device_id=(dom, 1 - rep), device_id_type=MESH)


class Copies:
    def __init__(self, send, recv):
        self.send, self.recv, self.used, self.open = send, recv, 0, []

    def take(self):
        self.used += 1
        return self.used - 1

    def start(self, number, src, dst, device):
        copy = pltpu.make_async_remote_copy(
            src_ref=src,
            dst_ref=dst,
            send_sem=self.send.at[number],
            recv_sem=self.recv.at[number],
            device_id=device,
            device_id_type=MESH,
        )
        copy.start()
        self.open.append(copy)

    def arrived(self, number, dst, device):
        pltpu.make_async_remote_copy(
            src_ref=dst,
            dst_ref=dst,
            send_sem=self.send.at[number],
            recv_sem=self.recv.at[number],
            device_id=device,
            device_id_type=MESH,
        ).wait_recv()

    def close(self):
        for copy in self.open:
            copy.wait_send()
        self.open = []


def one_hot(picks, counts, rows, base):
    nodes = picks[0].shape[1]
    row = lax.broadcasted_iota(jnp.int16, (rows, nodes), 0)
    table = jnp.zeros((rows, nodes), jnp.bfloat16)
    for pick, count in zip(picks, counts):
        here = jnp.broadcast_to(pick - base, (rows, nodes)).astype(jnp.int16)
        table = jnp.where(
            here == row, jnp.broadcast_to(count.astype(jnp.bfloat16), (rows, nodes)), table
        )
    return table


def ones_at(pick, rows, base=0):
    row = lax.broadcasted_iota(jnp.int32, (rows, pick.shape[1]), 0)
    return jnp.where(pick - base == row, 1.0, 0.0).astype(jnp.bfloat16)


def dot(a, b, over_a=1, over_b=0):
    return lax.dot_general(
        a, b, (((over_a,), (over_b,)), ((), ())), preferred_element_type=jnp.float32
    )


def side_by_side(rep, own, other, axis):
    first = jnp.where(rep == 0, own, other)
    second = jnp.where(rep == 0, other, own)
    return jnp.concatenate([first, second], axis=axis)


NORM = 131072.0**-0.5
N_COPIES = 420
PIECES = (0, 3, 1, 2)
ORDER = (2, 1, 3, 0)
BF, F32, I32 = jnp.bfloat16, jnp.float32, jnp.int32
SCRATCH = (
    [("g%d" % c, (4, 4, 4, UNIT, 128), BF) for c in range(3)]
    + [("x0", (4, 4, 2, UNIT, 128), BF), ("x1", (2, 4, 4, UNIT, 128), BF), ("x2", (4, 2, 4, UNIT, 128), BF)]
    + [("give0", (4, 4, 2, UNIT, 128), BF), ("give1", (2, 4, 4, UNIT, 128), BF)]
    + [("give2", (4, 2, 4, UNIT, 128), BF)]
    + [(name, (4, 4, 4, 1, 128), I32) for name in ("l1", "l2", "l3")]
    + [("featx", (1024, 128), BF), ("cotx", (1024, 128), BF), ("wsx", (128, 256), BF), ("wnx", (128, 256), BF)]
    + [("chooser", (2048, 288), BF), ("units", (288, 128), BF)]
    + [("picks", (16, 2048), I32), ("mult", (16, 2048), F32), ("table", (6144, 256), BF)]
    + [("total", (2048, 256), F32), ("totalx", (1024, 256), F32), ("grad", (2048, 256), BF)]
    + [("agg_send", (1024, 128), BF), ("out_send", (1024, 128), BF), ("agg_cols", (2048, 128), BF)]
    + [("terms", (4, 4, 4, 8, 128), F32), ("sums", (4, 4, 4, 8, 128), F32)]
    + [("local_sums", (2048, 256), BF)]
    + [("w1", (3, 4, 4, 8, 128), F32), ("w2", (3, 4, 8, 128), F32), ("wb", (4, 4, 8, 128), F32)]
    + [("wc", (4, 8, 128), F32), ("w3", (3, 8, 128), F32)]
    + [("r%d" % c, (2, UNIT, 128), F32) for c in range(3)]
    + [("whole%d" % c, (4, 4, 4, UNIT, 128), BF) for c in range(3)]
    + [("first%d" % c, (4, 4, UNIT, 128), BF) for c in range(3)]
    + [("second%d" % c, (4, UNIT, 128), BF) for c in range(3)]
    + [
        ("%s%d%d" % (stage, c, n), lead + ((shape[0] // 2,) + shape[1:] if n < 2 else shape), BF)
        for stage, lead, shape in (
            ("outer", (4,), (4, UNIT, 128)),
            ("middle", (), (4, UNIT, 128)),
            ("inner", (), (UNIT, 128)),
        )
        for c in range(3)
        for n in range(4)
    ]
)


def layer_kernel(*refs):
    (features, cotangent, self_weight, neighbor_weight, raw, brows, hrows, lists, counts) = refs[:9]
    output, gradient, grad_self, grad_neighbor = refs[9:13]
    named = {name: ref for (name, _, _), ref in zip(SCRATCH, refs[13:])}
    send, recv, local = refs[13 + len(SCRATCH) :]
    g0, g1, g2 = bufs = [named["g%d" % c] for c in range(3)]
    x0, x1, x2 = [named["x%d" % c] for c in range(3)]
    give0, give1, give2 = [named["give%d" % c] for c in range(3)]
    l1, l2, l3 = named["l1"], named["l2"], named["l3"]
    featx, cotx, wsx, wnx = named["featx"], named["cotx"], named["wsx"], named["wnx"]
    chooser, units, picks, mult = named["chooser"], named["units"], named["picks"], named["mult"]
    table, total, totalx, grad = named["table"], named["total"], named["totalx"], named["grad"]
    agg_send, out_send, agg_cols = named["agg_send"], named["out_send"], named["agg_cols"]
    terms, sums, local_sums = named["terms"], named["sums"], named["local_sums"]
    w1, w2, wb, wc, w3 = (named[name] for name in ("w1", "w2", "wb", "wc", "w3"))
    results = [named["r%d" % c] for c in range(3)]
    wholes = [named["whole%d" % c] for c in range(3)]
    firsts = [named["first%d" % c] for c in range(3)]
    seconds = [named["second%d" % c] for c in range(3)]
    outer_recv, middle_recv, inner_recv = (
        [[named["%s%d%d" % (stage, c, n)] for n in range(4)] for c in range(3)]
        for stage in ("outer", "middle", "inner")
    )
    dom, rep, at = place()
    other = (dom, 1 - rep)
    io = Copies(send, recv)
    signal_all(dom, rep, at)
    chooser[:, 0:256] = ones_at(brows[...], 2048)
    chooser[:, 256:288] = ones_at(hrows[...], 2048)
    units[...] = dot(chooser[...], features[...], 0, 0).astype(BF)
    pl.semaphore_wait(pltpu.get_barrier_semaphore(), 10)

    def prepare():
        halo = raw[8:12]
        end = jnp.int32(0)
        sender = jnp.zeros_like(halo)
        before = jnp.zeros_like(halo)
        for p in range(64):
            end = end + counts[0, p]
            passed = halo >= end
            sender = sender + jnp.where(passed, 1, 0)
            before = before + jnp.where(passed, counts[0, p], 0)
        sender = jnp.minimum(sender, 63)
        slot = jnp.clip(halo - before, 0, 127)

        def in_half(p, within, size):
            number = (p >> 2) * 2 + (p & 1)
            return jnp.where(((p & 3) >> 1) == rep, number * size + within, -1)

        hub = raw[12:16]
        local = raw[0:8] - rep * 1024
        local = jnp.where((local >= 0) & (local < 1024), local, -1)
        groups = (local, in_half(sender, slot, 128), in_half(hub >> 5, hub & 31, 32))
        start = 0
        for group in groups:
            size = group.shape[0]
            picks[start : start + size] = group
            for a in range(size):
                total = jnp.zeros((1, group.shape[1]), jnp.float32)
                for b in range(size):
                    total = total + jnp.where(group[a : a + 1] == group[b : b + 1], 1.0, 0.0)
                mult[start + a : start + a + 1] = total
            start += size

    def local_gather(tile):
        cols = slice(tile * 512, tile * 512 + 512)
        chosen = [picks[k : k + 1, cols] for k in range(8)]
        counts_of = [mult[k : k + 1, cols] for k in range(8)]
        total[cols] = dot(one_hot(chosen, counts_of, 512, 0), table[0:512], 0, 0) + dot(
            one_hot(chosen, counts_of, 512, 512), table[512:1024], 0, 0
        )

    coords = [tuple(at[a] for a in CHAINS[chain]) for chain in range(3)]
    ways = [
        [
            ((shifted(dom, at, a, 1), rep), (shifted(dom, at, a, 3), rep))
            for a in CHAINS[chain]
        ]
        for chain in range(3)
    ]

    inner_ids = [[io.take() for _ in range(4)] for _ in range(3)]
    mine = []
    for chain in range(3):
        o, m, i = coords[chain]
        up, down = ways[chain][2]
        io.start(inner_ids[chain][0], units.at[pl.ds(chain * UNIT, UNIT)], bufs[chain].at[o, m, i], up)
        io.start(inner_ids[chain][1], units.at[pl.ds(chain * UNIT, UNIT)], bufs[chain].at[o, m, i], down)
        copy = pltpu.make_async_copy(units.at[pl.ds(chain * UNIT, UNIT)], bufs[chain].at[o, m, i], local.at[chain])
        copy.start()
        mine.append(copy)

    list_steps = (
        ("y", lambda j: lists.at[j], lambda j: l1.at[j]),
        ("x", lambda j: l1.at[:, j], lambda j: l2.at[j]),
        ("z", lambda j: l2.at[:, :, j], lambda j: l3.at[j]),
    )
    list_ids = [[io.take() for _ in range(3)] for _ in range(3)]

    def send_lists(step):
        axis, src, dst = list_steps[step]
        for delta in (1, 2, 3):
            there = (at[axis] + delta) % 4
            io.start(
                list_ids[step][delta - 1],
                src(there),
                dst(at[axis]),
                (shifted(dom, at, axis, delta), rep),
            )
        copy = pltpu.make_async_copy(src(at[axis]), dst(at[axis]), local.at[3])
        copy.start()
        return copy

    def take_lists(step, copy):
        axis, _, dst = list_steps[step]
        copy.wait()
        for delta in (1, 2, 3):
            io.arrived(list_ids[step][delta - 1], dst((at[axis] - delta) % 4), other)

    theirs = pl.ds(pl.multiple_of((1 - rep) * 1024, 1024), 1024)
    pairs = (
        (features.at[theirs], featx),
        (self_weight, wsx),
        (neighbor_weight, wnx),
        (cotangent.at[theirs], cotx),
    )
    pair_ids = [io.take() for _ in pairs]
    for number, (src, dst) in zip(pair_ids, pairs):
        io.start(number, src, dst, other)
    listed = send_lists(0)
    prepare()

    swap0, swap1, swap2 = io.used, io.used + 16, io.used + 24
    io.used += 32

    def swap(chain, o, m):
        if chain == 0:
            pltpu.make_async_remote_copy(
                src_ref=g0.at[o, m, pl.ds(2 * (1 - rep), 2)],
                dst_ref=x0.at[o, m],
                send_sem=send.at[swap0 + o * 4 + m],
                recv_sem=recv.at[swap0 + o * 4 + m],
                device_id=other,
                device_id_type=MESH,
            ).start()
            return
        z = o if chain == 1 else m

        @pl.when(z // 2 != rep)
        def _():
            if chain == 1:
                number, dst = swap1 + (o % 2) * 4 + m, x1.at[o % 2, m]
            else:
                number, dst = swap2 + o * 2 + m % 2, x2.at[o, m % 2]
            pltpu.make_async_remote_copy(
                src_ref=bufs[chain].at[o, m],
                dst_ref=dst,
                send_sem=send.at[number],
                recv_sem=recv.at[number],
                device_id=other,
                device_id_type=MESH,
            ).start()

    middle_ids = [[io.take() for _ in range(4)] for _ in range(3)]
    outer_ids = [[[io.take() for _ in range(4)] for _ in range(4)] for _ in range(3)]

    def spread(chain, piece):
        o, m, _ = coords[chain]
        up, down = ways[chain][0]
        block = bufs[chain].at[o, (m + piece) % 4]
        ids = outer_ids[chain][piece]
        io.start(ids[0], block, block, up)
        io.start(ids[1], block, block, down)
        swap(chain, o, (m + piece) % 4)

    def pass_on(chain, ids, from_down, from_up, half, up, down):
        io.arrived(ids[0], from_down, down)
        io.start(ids[2], half(from_down, 0), half(from_down, 0), up)
        io.arrived(ids[1], from_up, up)
        io.start(ids[3], half(from_up, 1), half(from_up, 1), down)

    def rows_half(ref, which):
        return ref.at[pl.ds(which * (UNIT // 2), UNIT // 2)]

    def units_half(ref, which):
        return ref.at[pl.ds(which * 2, 2)]


    def inner_pass():
        for chain in range(3):
            o, m, i = coords[chain]
            up, down = ways[chain][2]
            buf = bufs[chain]
            pass_on(
                chain,
                inner_ids[chain],
                buf.at[o, m, (i + 3) % 4],
                buf.at[o, m, (i + 1) % 4],
                rows_half,
                up,
                down,
            )

    def inner_end():
        for chain in range(3):
            o, m, i = coords[chain]
            up, down = ways[chain][2]
            far = bufs[chain].at[o, m, (i + 2) % 4]
            mine[chain].wait()
            io.arrived(inner_ids[chain][2], rows_half(far, 0), down)
            io.arrived(inner_ids[chain][3], rows_half(far, 1), up)
            up, down = ways[chain][1]
            block = bufs[chain].at[o, m]
            io.start(middle_ids[chain][0], block, block, up)
            io.start(middle_ids[chain][1], block, block, down)
            spread(chain, 0)

    def middle_pass():
        for chain in range(3):
            o, m, i = coords[chain]
            up, down = ways[chain][1]
            buf = bufs[chain]
            pass_on(
                chain,
                middle_ids[chain],
                buf.at[o, (m + 3) % 4],
                buf.at[o, (m + 1) % 4],
                units_half,
                up,
                down,
            )
            spread(chain, 3)
            spread(chain, 1)

    def middle_end():
        for chain in range(3):
            o, m, i = coords[chain]
            up, down = ways[chain][1]
            far = bufs[chain].at[o, (m + 2) % 4]
            io.arrived(middle_ids[chain][2], units_half(far, 0), down)
            io.arrived(middle_ids[chain][3], units_half(far, 1), up)
            spread(chain, 2)

    def spread_pass(piece):
        for chain in range(3):
            o, m, i = coords[chain]
            up, down = ways[chain][0]
            buf, at_m = bufs[chain], (m + piece) % 4
            pass_on(
                chain,
                outer_ids[chain][piece],
                buf.at[(o + 3) % 4, at_m],
                buf.at[(o + 1) % 4, at_m],
                units_half,
                up,
                down,
            )
            swap(chain, (o + 3) % 4, at_m)
            swap(chain, (o + 1) % 4, at_m)

    def spread_end(piece):
        for chain in range(3):
            o, m, i = coords[chain]
            up, down = ways[chain][0]
            far = bufs[chain].at[(o + 2) % 4, (m + piece) % 4]
            io.arrived(outer_ids[chain][piece][2], units_half(far, 0), down)
            io.arrived(outer_ids[chain][piece][3], units_half(far, 1), up)
            swap(chain, (o + 2) % 4, (m + piece) % 4)

    inner_pass()
    inner_end()
    take_lists(0, listed)
    listed = send_lists(1)
    for number, (_, dst) in zip(pair_ids, pairs):
        io.arrived(number, dst, other)
    own_rows = pl.ds(pl.multiple_of(rep * 1024, 1024), 1024)
    table[0:1024] = side_by_side(rep, features[own_rows], featx[...], 1)
    local_gather(0)
    middle_pass()
    take_lists(1, listed)
    listed = send_lists(2)
    spread_pass(0)
    local_gather(1)
    middle_end()
    spread_end(0)
    spread_pass(3)
    local_gather(2)
    spread_pass(1)
    spread_end(3)
    local_gather(3)
    spread_pass(2)
    take_lists(2, listed)
    spread_end(1)
    spread_end(2)

    def settle(number, ref):
        copy = pltpu.make_async_remote_copy(
            src_ref=ref,
            dst_ref=ref,
            send_sem=send.at[number],
            recv_sem=recv.at[number],
            device_id=other,
            device_id_type=MESH,
        )
        copy.wait_recv()
        copy.wait_send()

    for a in range(4):
        for b in range(4):
            settle(swap0 + a * 4 + b, x0.at[a, b])
        for b in range(2):
            settle(swap1 + b * 4 + a, x1.at[b, a])
            settle(swap2 + a * 2 + b, x2.at[a, b])

    def select(number, carry):
        y, x, z = number // 8, (number // 2) % 4, number % 2
        zz = 2 * rep + z
        wide = [
            side_by_side(rep, own, came, 1)
            for own, came in (
                (g0[y, x, zz], x0[y, x, z]),
                (g1[zz, y, x], x1[z, y, x]),
                (g2[x, zz, y], x2[x, z, y]),
            )
        ]
        rows = jnp.concatenate([wide[0], wide[1], wide[2][:64]], axis=0)
        slots = dot(ones_at(l3[zz, x, y], 256), rows, 0, 0)
        table[pl.ds(pl.multiple_of(1024 + number * 128, 128), 128)] = slots.astype(jnp.bfloat16)
        table[pl.ds(pl.multiple_of(5120 + number * 32, 32), 32)] = wide[2][64:]
        return carry

    lax.fori_loop(0, 32, select, 0)

    def gather_tile(tile):
        cols = pl.ds(pl.multiple_of(tile * 512, 512), 512)
        value = total[cols]
        for first, some, begin, end in ((8, 4, 1024, 5120), (12, 4, 5120, 6144)):
            chosen = [picks[k : k + 1, cols] for k in range(first, first + some)]
            counts_of = [mult[k : k + 1, cols] for k in range(first, first + some)]
            for base in range(begin, end, 512):
                value = value + dot(
                    one_hot(chosen, counts_of, 512, base - begin), table[base : base + 512], 0, 0
                )
        total[cols] = value

    sums_at = io.used
    io.used += 2

    def sum_copy(k, tile):
        cols = pl.ds(pl.multiple_of(tile * 512, 512), 512)
        return pltpu.make_async_remote_copy(
            src_ref=total.at[cols],
            dst_ref=totalx.at[pl.ds(pl.multiple_of(k * 512, 512), 512)],
            send_sem=send.at[sums_at + k],
            recv_sem=recv.at[sums_at + k],
            device_id=other,
            device_id_type=MESH,
        )

    def gather_theirs(k, carry):
        gather_tile((1 - rep) * 2 + k)
        sum_copy(k, (1 - rep) * 2 + k).start()
        return carry

    def gather_mine(k, carry):
        gather_tile(rep * 2 + k)
        return carry

    lax.fori_loop(0, 2, gather_theirs, 0)
    lax.fori_loop(0, 2, gather_mine, 0)

    selfw = side_by_side(rep, self_weight[...], wsx[...], 0)
    nbrw = side_by_side(rep, neighbor_weight[...], wnx[...], 0)
    grad_ids = [[io.take() for _ in range(3)] for _ in range(2)]
    for step in range(4):
        if step % 2 == 0:
            sum_copy(step // 2, (1 - rep) * 2 + step // 2).wait_recv()
        rows = pl.ds(pl.multiple_of(rep * 1024 + step * 256, 256), 256)
        part = slice(step * 256, step * 256 + 256)
        wide = side_by_side(rep, features[rows], featx[part], 1)
        cotan = side_by_side(rep, cotangent[rows], cotx[part], 1)
        aggregate = ((total[rows] + totalx[part]) * (1.0 / 16.0)).astype(jnp.bfloat16)
        pre_act = dot(wide, selfw) + dot(aggregate, nbrw)
        sigmoid = 1.0 / (1.0 + jnp.exp(-pre_act))
        result = (pre_act * sigmoid).astype(jnp.bfloat16)
        slope = sigmoid * (1.0 + pre_act * (1.0 - sigmoid))
        grad[rows] = (cotan.astype(jnp.float32) * slope).astype(jnp.bfloat16)
        agg_send[part] = jnp.where(rep == 0, aggregate[:, 128:], aggregate[:, :128])
        out_send[part] = jnp.where(rep == 0, result[:, 128:], result[:, :128])
        agg_cols[rows] = jnp.where(rep == 0, aggregate[:, :128], aggregate[:, 128:])
        output[rows] = jnp.where(rep == 0, result[:, :128], result[:, 128:])
        if step % 2 == 1:
            n = grad_ids[step // 2]
            tall = pl.ds(pl.multiple_of(rep * 1024 + (step // 2) * 512, 512), 512)
            flat = pl.ds((step // 2) * 512, 512)
            io.start(n[0], grad.at[tall], grad.at[tall], other)
            io.start(n[1], agg_send.at[flat], agg_cols.at[tall], other)
            io.start(n[2], out_send.at[flat], output.at[tall], other)
    for k in range(2):
        sum_copy(k, (1 - rep) * 2 + k).wait_send()

    own_terms = (
        dot(features[own_rows], grad[own_rows], 0, 0),
        dot(agg_cols[own_rows], grad[own_rows], 0, 0),
    )
    for k in range(2):
        tall = pl.ds(pl.multiple_of((1 - rep) * 1024 + k * 512, 512), 512)
        io.arrived(grad_ids[k][0], grad.at[tall], other)
        io.arrived(grad_ids[k][1], agg_cols.at[tall], other)
    for n, (mine_term, data) in enumerate(zip(own_terms, (features, agg_cols))):
        term = mine_term + dot(data[theirs], grad[theirs], 0, 0)
        for h in range(2):
            for b in range(16):
                terms[2 * n + h, b // 4, b % 4] = term[b * 8 : b * 8 + 8, h * 128 : h * 128 + 128]

    def scatter_step(step, carry):
        sums_of = jnp.zeros((640, 256), jnp.float32)
        for begin in range(0, 2048, 256):
            cols = slice(begin, begin + 256)
            parts = []
            for first, some, rows in ((8, 4, 512), (12, 4, 128)):
                chosen = [picks[k : k + 1, cols] for k in range(first, first + some)]
                counts_of = [mult[k : k + 1, cols] for k in range(first, first + some)]
                parts.append(one_hot(chosen, counts_of, rows, step * rows))
            sums_of = sums_of + dot(jnp.concatenate(parts, axis=0), grad[cols])
        slots = sums_of[0:512].astype(jnp.bfloat16)
        hubs = sums_of[512:640].astype(jnp.bfloat16)
        for k in range(4):
            y, x, z = step // 2, (step % 2) * 2 + k // 2, k % 2
            zz = 2 * rep + z
            rows = dot(ones_at(l3[zz, x, y], 256), slots[k * 128 : k * 128 + 128])
            rows = rows.astype(jnp.bfloat16)
            rows = jnp.concatenate([rows, hubs[k * 32 : k * 32 + 32]], axis=0)
            keep = jnp.where(rep == 0, rows[:, :128], rows[:, 128:])
            give = jnp.where(rep == 0, rows[:, 128:], rows[:, :128])
            wholes[0][y, x, zz], give0[y, x, z] = keep[0:96], give[0:96]
            wholes[1][zz, y, x], give1[z, y, x] = keep[96:192], give[96:192]
            wholes[2][x, zz, y], give2[x, z, y] = keep[192:288], give[192:288]
        return carry

    def output_done():
        for k in range(2):
            tall = pl.ds(pl.multiple_of((1 - rep) * 1024 + k * 512, 512), 512)
            io.arrived(grad_ids[k][2], output.at[tall], other)

    def trade(axis, src, dst):
        ids = [io.take() for _ in range(3)]
        for delta in (1, 2, 3):
            device = (shifted(dom, at, axis, delta), rep)
            io.start(ids[delta - 1], src(delta), dst(delta), device)
        return ids

    def traded(ids, dst):
        for delta in (1, 2, 3):
            io.arrived(ids[delta - 1], dst(delta), other)

    def reduce_start(axis, src, landing):
        return trade(axis, lambda d: src.at[(at[axis] + d) % 4], lambda d: landing.at[d - 1])

    def reduce_end(ids, src, axis, landing):
        traded(ids, lambda d: landing.at[d - 1])
        return src[at[axis]] + landing[0] + landing[1] + landing[2]

    def give_start(axis, ref):
        return trade(axis, lambda d: ref(at[axis]), lambda d: ref(at[axis]))

    def give_end(ids, axis, ref):
        traded(ids, lambda d: ref((at[axis] - d) % 4))

    gives = {
        "z": lambda j: sums.at[at["y"], at["x"], j],
        "x": lambda j: sums.at[at["y"], j],
        "y": lambda j: sums.at[j],
    }

    swap_ids = [[io.take() for _ in range(4)] for _ in range(3)]

    def swap_refs(chain, piece, half):
        m = (coords[chain][1] + piece) % 4
        span = pl.ds(2 * half, 2)
        if chain == 0:
            return give0.at[:, m], wholes[0].at[:, m, span]
        if chain == 1:
            return give1.at[:, m], wholes[1].at[span, m]
        return give2.at[:, m % 2], wholes[2].at[:, m]

    def remote(number, src, dst):
        return pltpu.make_async_remote_copy(
            src_ref=src,
            dst_ref=dst,
            send_sem=send.at[number],
            recv_sem=recv.at[number],
            device_id=other,
            device_id_type=MESH,
        )

    def swap_start(chain, piece):
        number = swap_ids[chain][piece]
        src, dst = swap_refs(chain, piece, rep)

        def go():
            remote(number, src, dst).start()

        if chain == 2:
            pl.when((coords[2][1] + piece) % 4 // 2 == rep)(go)
        else:
            go()

    def swap_end(chain, piece):
        number = swap_ids[chain][piece]
        src, dst = swap_refs(chain, piece, rep)
        _, came = swap_refs(chain, piece, 1 - rep)

        def kept():
            remote(number, src, dst).wait_send()

        def got():
            remote(number, came, came).wait_recv()

        if chain == 2:
            here = (coords[2][1] + piece) % 4 // 2 == rep
            pl.when(here)(kept)
            pl.when(jnp.logical_not(here))(got)
        else:
            kept()
            got()


    weigh = reduce_start("y", terms, w1)
    lax.fori_loop(0, 8, scatter_step, 0)
    for piece in ORDER:
        for chain in range(3):
            swap_start(chain, piece)

    outer_ids = [[[io.take() for _ in range(6)] for _ in range(4)] for _ in range(3)]
    middle_ids = [[io.take() for _ in range(6)] for _ in range(3)]
    inner_ids = [[io.take() for _ in range(6)] for _ in range(3)]
    low2, high2 = pl.ds(0, 2), pl.ds(2, 2)
    lowr, highr = pl.ds(0, UNIT // 2), pl.ds(UNIT // 2, UNIT // 2)

    def add_into(spot, came):
        spot[...] = (spot[...].astype(jnp.float32) + came[...].astype(jnp.float32)).astype(jnp.bfloat16)

    def three(a, b, c):
        return a[...].astype(jnp.float32) + b[...].astype(jnp.float32) + c[...].astype(jnp.float32)

    def outer_start(piece):
        for chain in range(3):
            swap_end(chain, piece)
            o, m, i = coords[chain]
            up, down = ways[chain][0]
            data, m = wholes[chain], (m + piece) % 4
            from_low, from_high, whole_low, whole_high = (r.at[piece] for r in outer_recv[chain])
            n = outer_ids[chain][piece]
            io.start(n[0], data.at[(o + 2) % 4, m, low2], from_low, up)
            io.start(n[1], data.at[(o + 2) % 4, m, high2], from_high, down)
            io.start(n[2], data.at[(o + 1) % 4, m, high2], whole_low.at[high2], up)
            io.start(n[3], data.at[(o + 3) % 4, m, low2], whole_high.at[low2], down)

    def outer_pass(piece):
        for chain in range(3):
            o, m, i = coords[chain]
            up, down = ways[chain][0]
            data, m = wholes[chain], (m + piece) % 4
            from_low, from_high, whole_low, whole_high = (r.at[piece] for r in outer_recv[chain])
            n = outer_ids[chain][piece]
            io.arrived(n[0], from_low, other)
            for k in range(2):
                add_into(data.at[(o + 1) % 4, m, k], from_low.at[k])
            io.start(n[4], data.at[(o + 1) % 4, m, low2], whole_low.at[low2], up)
            io.arrived(n[1], from_high, other)
            for k in range(2):
                add_into(data.at[(o + 3) % 4, m, 2 + k], from_high.at[k])
            io.start(n[5], data.at[(o + 3) % 4, m, high2], whole_high.at[high2], down)

    def outer_end(piece):
        for chain in range(3):
            o, m, i = coords[chain]
            data, target = wholes[chain], firsts[chain].at[piece]
            _, _, whole_low, whole_high = (r.at[piece] for r in outer_recv[chain])
            n = outer_ids[chain][piece]
            io.arrived(n[2], whole_low.at[high2], other)
            io.arrived(n[3], whole_high.at[low2], other)
            io.arrived(n[4], whole_low.at[low2], other)
            io.arrived(n[5], whole_high.at[high2], other)
            for k in range(4):
                target[k] = three(
                    data.at[o, (m + piece) % 4, k], whole_low.at[k], whole_high.at[k]
                ).astype(jnp.bfloat16)
            up, down = ways[chain][1]
            from_low, from_high, whole_low, whole_high = middle_recv[chain]
            n = middle_ids[chain]
            if piece == 2:
                io.start(n[0], target.at[low2], from_low, up)
                io.start(n[1], target.at[high2], from_high, down)
            if piece == 1:
                io.start(n[2], target.at[high2], whole_low.at[high2], up)
            if piece == 3:
                io.start(n[3], target.at[low2], whole_high.at[low2], down)


    local_ids = [io.take() for _ in range(4)]

    def local_scatter(part):
        value = jnp.zeros((256, 256), jnp.float32)
        for begin in range(0, 2048, 512):
            cols = slice(begin, begin + 512)
            chosen = [picks[k : k + 1, cols] for k in range(8)]
            counts_of = [mult[k : k + 1, cols] for k in range(8)]
            value = value + dot(one_hot(chosen, counts_of, 256, part * 256), grad[cols])
        rows = pl.ds(pl.multiple_of(rep * 1024 + part * 256, 256), 256)
        local_sums[rows] = (value * (1.0 / 16.0)).astype(jnp.bfloat16)
        io.start(local_ids[part], local_sums.at[rows], local_sums.at[rows], other)

    def products(half):
        if half == 0:
            for part in range(4):
                rows = pl.ds(pl.multiple_of((1 - rep) * 1024 + part * 256, 256), 256)
                io.arrived(local_ids[part], local_sums.at[rows], other)
        for begin in range(half * 1024, half * 1024 + 1024, 512):
            rows = slice(begin, begin + 512)
            total[rows, 0:128] = dot(grad[rows], self_weight[...], 1, 1) + dot(
                local_sums[rows], neighbor_weight[...], 1, 1
            )

    outer_start(2)
    wb[...] = reduce_end(weigh, terms, "y", w1)
    weigh = reduce_start("x", wb, w2)
    outer_start(1)
    outer_pass(2)
    wc[...] = reduce_end(weigh, wb, "x", w2)
    weigh = reduce_start("z", wc, w3)
    outer_start(3)
    local_scatter(0)
    outer_pass(1)
    sums[at["y"], at["x"], at["z"]] = reduce_end(weigh, wc, "z", w3)
    weigh = give_start("z", gives["z"])
    outer_end(2)
    outer_start(0)
    local_scatter(1)
    outer_pass(3)
    outer_end(1)
    give_end(weigh, "z", gives["z"])
    weigh = give_start("x", gives["x"])
    outer_pass(0)
    local_scatter(2)
    outer_end(3)
    for chain in range(3):
        up, down = ways[chain][1]
        from_low, from_high, whole_low, whole_high = middle_recv[chain]
        n = middle_ids[chain]
        io.arrived(n[0], from_low, other)
        for k in range(2):
            add_into(firsts[chain].at[1, k], from_low.at[k])
        io.start(n[4], firsts[chain].at[1, low2], whole_low.at[low2], up)
        io.arrived(n[1], from_high, other)
        for k in range(2):
            add_into(firsts[chain].at[3, 2 + k], from_high.at[k])
        io.start(n[5], firsts[chain].at[3, high2], whole_high.at[high2], down)
    local_scatter(3)
    outer_end(0)
    give_end(weigh, "x", gives["x"])
    weigh = give_start("y", gives["y"])
    for chain in range(3):
        o, m, i = coords[chain]
        from_low, from_high, whole_low, whole_high = middle_recv[chain]
        n = middle_ids[chain]
        io.arrived(n[2], whole_low.at[high2], other)
        io.arrived(n[3], whole_high.at[low2], other)
        io.arrived(n[4], whole_low.at[low2], other)
        io.arrived(n[5], whole_high.at[high2], other)
        target = seconds[chain]
        for k in range(4):
            target[k] = three(firsts[chain].at[0, k], whole_low.at[k], whole_high.at[k]).astype(
                jnp.bfloat16
            )
        up, down = ways[chain][2]
        from_low, from_high, whole_low, whole_high = inner_recv[chain]
        n = inner_ids[chain]
        io.start(n[0], target.at[(i + 2) % 4, lowr], from_low, up)
        io.start(n[1], target.at[(i + 2) % 4, highr], from_high, down)
        io.start(n[2], target.at[(i + 1) % 4, highr], whole_low.at[highr], up)
        io.start(n[3], target.at[(i + 3) % 4, lowr], whole_high.at[lowr], down)
    for chain in range(3):
        o, m, i = coords[chain]
        up, down = ways[chain][2]
        target = seconds[chain]
        from_low, from_high, whole_low, whole_high = inner_recv[chain]
        n = inner_ids[chain]
        io.arrived(n[0], from_low, other)
        add_into(target.at[(i + 1) % 4, lowr], from_low)
        io.start(n[4], target.at[(i + 1) % 4, lowr], whole_low.at[lowr], up)
        io.arrived(n[1], from_high, other)
        add_into(target.at[(i + 3) % 4, highr], from_high)
        io.start(n[5], target.at[(i + 3) % 4, highr], whole_high.at[highr], down)
    products(0)
    products(1)
    last = [io.take() for _ in range(3)]
    for chain in range(3):
        o, m, i = coords[chain]
        from_low, from_high, whole_low, whole_high = inner_recv[chain]
        n = inner_ids[chain]
        io.arrived(n[2], whole_low.at[highr], other)
        io.arrived(n[3], whole_high.at[lowr], other)
        io.arrived(n[4], whole_low.at[lowr], other)
        io.arrived(n[5], whole_high.at[highr], other)
        results[chain][rep] = three(seconds[chain].at[i], whole_low, whole_high)
        io.start(last[chain], results[chain].at[rep], results[chain].at[rep], other)
    give_end(weigh, "y", gives["y"])
    for chain in range(3):
        io.arrived(last[chain], results[chain].at[1 - rep], other)
    output_done()
    tall = jnp.concatenate(
        [jnp.concatenate([r[0], r[1]], axis=1) for r in results], axis=0
    )
    value = dot((tall * (1.0 / 16.0)).astype(jnp.bfloat16), neighbor_weight[...], 1, 1)
    high = value.astype(jnp.bfloat16)
    low = (value - high.astype(jnp.float32)).astype(jnp.bfloat16)
    for begin in range(0, 2048, 512):
        rows = slice(begin, begin + 512)
        gradient[rows] = (
            total[rows, 0:128] + dot(chooser[rows], high) + dot(chooser[rows], low)
        ).astype(jnp.bfloat16)
    for n, target in enumerate((grad_self, grad_neighbor)):
        for h in range(2):
            for b in range(16):
                target[b * 8 : b * 8 + 8, h * 128 : h * 128 + 128] = (
                    sums[2 * n + h, b // 4, b % 4] * NORM
                )
    io.close()


def layer_call(features, cotangent, self_weight, neighbor_weight, raw, brows, hrows, lists, counts):
    args = (features, cotangent, self_weight, neighbor_weight, raw, brows, hrows, lists, counts)
    return pl.pallas_call(
        layer_kernel,
        out_shape=[jax.ShapeDtypeStruct((2048, 128), BF)] * 2
        + [jax.ShapeDtypeStruct((128, 256), F32)] * 2,
        in_specs=[VMEM_SPEC] * 8 + [pl.BlockSpec(memory_space=pltpu.SMEM)],
        out_specs=[VMEM_SPEC] * 4,
        scratch_shapes=[pltpu.VMEM(shape, kind) for _, shape, kind in SCRATCH]
        + [
            pltpu.SemaphoreType.DMA((N_COPIES,)),
            pltpu.SemaphoreType.DMA((N_COPIES,)),
            pltpu.SemaphoreType.DMA((4,)),
        ],
        compiler_params=pltpu.CompilerParams(
            collective_id=0, has_side_effects=True, vmem_limit_bytes=BIG
        ),
        name="layer",
    )(*args)


def per_device(
    features,
    cotangent,
    self_weight,
    neighbor_weight,
    local_neighbors,
    hub_rows,
    hub_neighbors,
    boundary_rows,
    send_lists,
    received_counts,
    halo_neighbors,
):
    raw = jnp.concatenate([local_neighbors.T, halo_neighbors.T, hub_neighbors.T], axis=0)
    output, gradient, grad_self, grad_neighbor = layer_call(
        features,
        cotangent,
        self_weight,
        neighbor_weight,
        raw,
        boundary_rows[None],
        hub_rows[None],
        send_lists.reshape(4, 4, 4, 1, 128),
        received_counts,
    )
    return output, gradient, grad_self, grad_neighbor


def solution(mesh):
    return jax.shard_map(
        per_device,
        mesh=mesh,
        in_specs=(
            P("dom", "rep"),
            P("dom", "rep"),
            P("rep", None),
            P("rep", None),
            P("dom", None),
            P("dom"),
            P("dom", None),
            P("dom"),
            P("dom", None, None),
            P("dom", None),
            P("dom", None),
        ),
        out_specs=(P("dom", "rep"), P("dom", "rep"), P("rep", None), P("rep", None)),
        check_vma=False,
    )
```

```python
import functools

import jax
import jax.numpy as jnp
from jax import lax
from jax.experimental import pallas as pl
from jax.experimental.pallas import tpu as pltpu
from jax.sharding import PartitionSpec as P

MESH = pl.DeviceIdType.MESH
VMEM_SPEC = pl.BlockSpec(memory_space=pltpu.VMEM)
STRIDE = {"y": 16, "x": 4, "z": 1}
CHAINS = (("y", "x", "z"), ("z", "y", "x"), ("x", "z", "y"))
UNIT = 96
SHARE = (80, 128, 80)
SHARE_AT = (0, 80, 208)
BIG = 58 * 2**20


def place():
    dom = lax.axis_index("dom")
    rep = lax.axis_index("rep")
    at = {"y": dom // 16, "x": (dom // 4) % 4, "z": dom % 4}
    return dom, rep, at


def shifted(dom, at, axis, delta):
    there = (at[axis] + delta) % 4
    return dom + (there - at[axis]) * STRIDE[axis]


def signal_all(dom, rep, at):
    barrier = pltpu.get_barrier_semaphore()
    for axis in "yxz":
        for delta in (1, 2, 3):
            pl.semaphore_signal(
                barrier, inc=1, device_id=(shifted(dom, at, axis, delta), rep), device_id_type=MESH
            )
    pl.semaphore_signal(barrier, inc=1, device_id=(dom, 1 - rep), device_id_type=MESH)


class Copies:
    def __init__(self, send, recv):
        self.send, self.recv, self.used, self.open = send, recv, 0, []

    def take(self):
        self.used += 1
        return self.used - 1

    def start(self, number, src, dst, device):
        copy = pltpu.make_async_remote_copy(
            src_ref=src,
            dst_ref=dst,
            send_sem=self.send.at[number],
            recv_sem=self.recv.at[number],
            device_id=device,
            device_id_type=MESH,
        )
        copy.start()
        self.open.append(copy)

    def arrived(self, number, dst, device):
        pltpu.make_async_remote_copy(
            src_ref=dst,
            dst_ref=dst,
            send_sem=self.send.at[number],
            recv_sem=self.recv.at[number],
            device_id=device,
            device_id_type=MESH,
        ).wait_recv()

    def close(self):
        for copy in self.open:
            copy.wait_send()
        self.open = []


def one_hot(picks, counts, rows, base):
    nodes = picks[0].shape[1]
    row = lax.broadcasted_iota(jnp.int16, (rows, nodes), 0)
    table = jnp.zeros((rows, nodes), jnp.bfloat16)
    for pick, count in zip(picks, counts):
        here = jnp.broadcast_to(pick - base, (rows, nodes)).astype(jnp.int16)
        table = jnp.where(
            here == row, jnp.broadcast_to(count.astype(jnp.bfloat16), (rows, nodes)), table
        )
    return table


def ones_at(pick, rows, base=0):
    row = lax.broadcasted_iota(jnp.int32, (rows, pick.shape[1]), 0)
    return jnp.where(pick - base == row, 1.0, 0.0).astype(jnp.bfloat16)


def dot(a, b, over_a=1, over_b=0):
    return lax.dot_general(
        a, b, (((over_a,), (over_b,)), ((), ())), preferred_element_type=jnp.float32
    )


def side_by_side(rep, own, other, axis):
    first = jnp.where(rep == 0, own, other)
    second = jnp.where(rep == 0, other, own)
    return jnp.concatenate([first, second], axis=axis)


NORM = 131072.0**-0.5
N_COPIES = 420
PIECES = (0, 3, 1, 2)
ORDER = (2, 1, 3, 0)
BF, F32, I32 = jnp.bfloat16, jnp.float32, jnp.int32
SCRATCH = (
    [("g%d" % c, (4, 4, 4, UNIT, 128), BF) for c in range(3)]
    + [("x0", (4, 4, 2, UNIT, 128), BF), ("x1", (2, 4, 4, UNIT, 128), BF), ("x2", (4, 2, 4, UNIT, 128), BF)]
    + [("give0", (4, 4, 2, SHARE[0], 128), BF), ("give1", (2, 4, 4, SHARE[1], 128), BF)]
    + [("give2", (4, 2, 4, SHARE[2], 128), BF)]
    + [(name, (4, 4, 4, 1, 128), I32) for name in ("l1", "l2", "l3")]
    + [("featx", (1024, 128), BF), ("cotx", (1024, 128), BF), ("wsx", (128, 256), BF), ("wnx", (128, 256), BF)]
    + [("chooser", (2048, 288), BF), ("units", (288, 128), BF)]
    + [("picks", (16, 2048), I32), ("mult", (16, 2048), F32), ("table", (6144, 256), BF)]
    + [("total", (2048, 256), F32), ("totalx", (1024, 256), F32), ("grad", (2048, 256), BF)]
    + [("agg_send", (1024, 128), BF), ("out_send", (1024, 128), BF), ("agg_cols", (2048, 128), BF)]
    + [("terms", (4, 4, 4, 8, 128), F32), ("sums", (4, 4, 4, 8, 128), F32)]
    + [("local_sums", (2048, 256), BF)]
    + [("w1", (3, 4, 4, 8, 128), F32), ("w2", (3, 4, 8, 128), F32), ("wb", (4, 4, 8, 128), F32)]
    + [("wc", (4, 8, 128), F32), ("w3", (3, 8, 128), F32)]
    + [("r%d" % c, (2, SHARE[c], 128), F32) for c in range(3)]
    + [("whole%d" % c, (4, 4, 4, SHARE[c], 128), BF) for c in range(3)]
    + [("first%d" % c, (4, 4, SHARE[c], 128), BF) for c in range(3)]
    + [("second%d" % c, (4, SHARE[c], 128), BF) for c in range(3)]
    + [("inner%d" % c, (3, SHARE[c], 128), BF) for c in range(3)]
    + [
        ("%s%d%d" % (stage, c, n), lead + (2 if n < 2 else 4, SHARE[c], 128), BF)
        for stage, lead in (("outer", (4,)), ("middle", ()))
        for c in range(3)
        for n in range(4)
    ]
)


def layer_kernel(*refs):
    (features, cotangent, self_weight, neighbor_weight, raw, brows, hrows, lists, counts) = refs[:9]
    output, gradient, grad_self, grad_neighbor = refs[9:13]
    named = {name: ref for (name, _, _), ref in zip(SCRATCH, refs[13:])}
    send, recv, local = refs[13 + len(SCRATCH) :]
    g0, g1, g2 = bufs = [named["g%d" % c] for c in range(3)]
    x0, x1, x2 = [named["x%d" % c] for c in range(3)]
    give0, give1, give2 = [named["give%d" % c] for c in range(3)]
    l1, l2, l3 = named["l1"], named["l2"], named["l3"]
    featx, cotx, wsx, wnx = named["featx"], named["cotx"], named["wsx"], named["wnx"]
    chooser, units, picks, mult = named["chooser"], named["units"], named["picks"], named["mult"]
    table, total, totalx, grad = named["table"], named["total"], named["totalx"], named["grad"]
    agg_send, out_send, agg_cols = named["agg_send"], named["out_send"], named["agg_cols"]
    terms, sums, local_sums = named["terms"], named["sums"], named["local_sums"]
    w1, w2, wb, wc, w3 = (named[name] for name in ("w1", "w2", "wb", "wc", "w3"))
    results = [named["r%d" % c] for c in range(3)]
    wholes = [named["whole%d" % c] for c in range(3)]
    firsts = [named["first%d" % c] for c in range(3)]
    seconds = [named["second%d" % c] for c in range(3)]
    outer_recv, middle_recv = (
        [[named["%s%d%d" % (stage, c, n)] for n in range(4)] for c in range(3)]
        for stage in ("outer", "middle")
    )
    inner_recv = [named["inner%d" % c] for c in range(3)]
    dom, rep, at = place()
    other = (dom, 1 - rep)
    io = Copies(send, recv)
    signal_all(dom, rep, at)
    chooser[:, 0:256] = ones_at(brows[...], 2048)
    chooser[:, 256:288] = ones_at(hrows[...], 2048)
    units[...] = dot(chooser[...], features[...], 0, 0).astype(BF)
    pl.semaphore_wait(pltpu.get_barrier_semaphore(), 10)

    def prepare():
        halo = raw[8:12]
        end = jnp.int32(0)
        sender = jnp.zeros_like(halo)
        before = jnp.zeros_like(halo)
        for p in range(64):
            end = end + counts[0, p]
            passed = halo >= end
            sender = sender + jnp.where(passed, 1, 0)
            before = before + jnp.where(passed, counts[0, p], 0)
        sender = jnp.minimum(sender, 63)
        slot = jnp.clip(halo - before, 0, 127)

        def in_half(p, within, size):
            number = (p >> 2) * 2 + (p & 1)
            return jnp.where(((p & 3) >> 1) == rep, number * size + within, -1)

        hub = raw[12:16]
        local = raw[0:8] - rep * 1024
        local = jnp.where((local >= 0) & (local < 1024), local, -1)
        groups = (local, in_half(sender, slot, 128), in_half(hub >> 5, hub & 31, 32))
        start = 0
        for group in groups:
            size = group.shape[0]
            picks[start : start + size] = group
            for a in range(size):
                total = jnp.zeros((1, group.shape[1]), jnp.float32)
                for b in range(size):
                    total = total + jnp.where(group[a : a + 1] == group[b : b + 1], 1.0, 0.0)
                mult[start + a : start + a + 1] = total
            start += size

    def local_gather(tile):
        cols = slice(tile * 512, tile * 512 + 512)
        chosen = [picks[k : k + 1, cols] for k in range(8)]
        counts_of = [mult[k : k + 1, cols] for k in range(8)]
        total[cols] = dot(one_hot(chosen, counts_of, 512, 0), table[0:512], 0, 0) + dot(
            one_hot(chosen, counts_of, 512, 512), table[512:1024], 0, 0
        )

    coords = [tuple(at[a] for a in CHAINS[chain]) for chain in range(3)]
    ways = [
        [
            ((shifted(dom, at, a, 1), rep), (shifted(dom, at, a, 3), rep))
            for a in CHAINS[chain]
        ]
        for chain in range(3)
    ]

    inner_ids = [[io.take() for _ in range(3)] for _ in range(3)]
    mine = []
    for chain in range(3):
        o, m, i = coords[chain]
        unit = units.at[pl.ds(chain * UNIT, UNIT)]
        for delta in (1, 3, 2):
            device = (shifted(dom, at, CHAINS[chain][2], delta), rep)
            io.start(inner_ids[chain][delta - 1], unit, bufs[chain].at[o, m, i], device)
        copy = pltpu.make_async_copy(unit, bufs[chain].at[o, m, i], local.at[chain])
        copy.start()
        mine.append(copy)

    list_steps = (
        ("y", lambda j: lists.at[j], lambda j: l1.at[j]),
        ("x", lambda j: l1.at[:, j], lambda j: l2.at[j]),
        ("z", lambda j: l2.at[:, :, j], lambda j: l3.at[j]),
    )
    list_ids = [[io.take() for _ in range(3)] for _ in range(3)]

    def send_lists(step):
        axis, src, dst = list_steps[step]
        for delta in (1, 2, 3):
            there = (at[axis] + delta) % 4
            io.start(
                list_ids[step][delta - 1],
                src(there),
                dst(at[axis]),
                (shifted(dom, at, axis, delta), rep),
            )
        copy = pltpu.make_async_copy(src(at[axis]), dst(at[axis]), local.at[3])
        copy.start()
        return copy

    def take_lists(step, copy):
        axis, _, dst = list_steps[step]
        copy.wait()
        for delta in (1, 2, 3):
            io.arrived(list_ids[step][delta - 1], dst((at[axis] - delta) % 4), other)

    theirs = pl.ds(pl.multiple_of((1 - rep) * 1024, 1024), 1024)
    pairs = (
        (features.at[theirs], featx),
        (self_weight, wsx),
        (neighbor_weight, wnx),
        (cotangent.at[theirs], cotx),
    )
    pair_ids = [io.take() for _ in pairs]
    for number, (src, dst) in zip(pair_ids, pairs):
        io.start(number, src, dst, other)
    listed = send_lists(0)

    swap0, swap1, swap2 = io.used, io.used + 16, io.used + 24
    io.used += 32

    def swap(chain, o, m):
        if chain == 0:
            pltpu.make_async_remote_copy(
                src_ref=g0.at[o, m, pl.ds(2 * (1 - rep), 2)],
                dst_ref=x0.at[o, m],
                send_sem=send.at[swap0 + o * 4 + m],
                recv_sem=recv.at[swap0 + o * 4 + m],
                device_id=other,
                device_id_type=MESH,
            ).start()
            return
        z = o if chain == 1 else m

        @pl.when(z // 2 != rep)
        def _():
            if chain == 1:
                number, dst = swap1 + (o % 2) * 4 + m, x1.at[o % 2, m]
            else:
                number, dst = swap2 + o * 2 + m % 2, x2.at[o, m % 2]
            pltpu.make_async_remote_copy(
                src_ref=bufs[chain].at[o, m],
                dst_ref=dst,
                send_sem=send.at[number],
                recv_sem=recv.at[number],
                device_id=other,
                device_id_type=MESH,
            ).start()

    middle_ids = [[io.take() for _ in range(4)] for _ in range(3)]
    outer_ids = [[[io.take() for _ in range(4)] for _ in range(4)] for _ in range(3)]

    def spread(chain, piece):
        o, m, _ = coords[chain]
        up, down = ways[chain][0]
        block = bufs[chain].at[o, (m + piece) % 4]
        ids = outer_ids[chain][piece]
        io.start(ids[0], block, block, up)
        io.start(ids[1], block, block, down)
        swap(chain, o, (m + piece) % 4)

    def pass_on(chain, ids, from_down, from_up, half, up, down):
        io.arrived(ids[0], from_down, down)
        io.start(ids[2], half(from_down, 0), half(from_down, 0), up)
        io.arrived(ids[1], from_up, up)
        io.start(ids[3], half(from_up, 1), half(from_up, 1), down)

    def units_half(ref, which):
        return ref.at[pl.ds(which * 2, 2)]


    def inner_end():
        for chain in range(3):
            o, m, i = coords[chain]
            mine[chain].wait()
            for delta in (1, 3, 2):
                io.arrived(inner_ids[chain][delta - 1], bufs[chain].at[o, m, (i - delta) % 4], other)
            up, down = ways[chain][1]
            block = bufs[chain].at[o, m]
            io.start(middle_ids[chain][0], block, block, up)
            io.start(middle_ids[chain][1], block, block, down)
            spread(chain, 0)

    def middle_pass():
        for chain in range(3):
            o, m, i = coords[chain]
            up, down = ways[chain][1]
            buf = bufs[chain]
            pass_on(
                chain,
                middle_ids[chain],
                buf.at[o, (m + 3) % 4],
                buf.at[o, (m + 1) % 4],
                units_half,
                up,
                down,
            )
            spread(chain, 3)
            spread(chain, 1)

    def middle_end():
        for chain in range(3):
            o, m, i = coords[chain]
            up, down = ways[chain][1]
            far = bufs[chain].at[o, (m + 2) % 4]
            io.arrived(middle_ids[chain][2], units_half(far, 0), down)
            io.arrived(middle_ids[chain][3], units_half(far, 1), up)
            spread(chain, 2)

    def spread_pass(piece):
        for chain in range(3):
            o, m, i = coords[chain]
            up, down = ways[chain][0]
            buf, at_m = bufs[chain], (m + piece) % 4
            pass_on(
                chain,
                outer_ids[chain][piece],
                buf.at[(o + 3) % 4, at_m],
                buf.at[(o + 1) % 4, at_m],
                units_half,
                up,
                down,
            )
            swap(chain, (o + 3) % 4, at_m)
            swap(chain, (o + 1) % 4, at_m)

    def spread_end(piece):
        for chain in range(3):
            o, m, i = coords[chain]
            up, down = ways[chain][0]
            far = bufs[chain].at[(o + 2) % 4, (m + piece) % 4]
            io.arrived(outer_ids[chain][piece][2], units_half(far, 0), down)
            io.arrived(outer_ids[chain][piece][3], units_half(far, 1), up)
            swap(chain, (o + 2) % 4, (m + piece) % 4)

    inner_end()
    prepare()
    take_lists(0, listed)
    listed = send_lists(1)
    for number, (_, dst) in zip(pair_ids, pairs):
        io.arrived(number, dst, other)
    own_rows = pl.ds(pl.multiple_of(rep * 1024, 1024), 1024)
    table[0:1024] = side_by_side(rep, features[own_rows], featx[...], 1)
    middle_pass()
    take_lists(1, listed)
    listed = send_lists(2)
    spread_pass(0)
    middle_end()
    local_gather(0)
    spread_end(0)
    spread_pass(3)
    local_gather(1)
    spread_pass(1)
    local_gather(2)
    spread_end(3)
    spread_pass(2)
    local_gather(3)
    take_lists(2, listed)
    spread_end(1)
    spread_end(2)

    def settle(number, ref):
        copy = pltpu.make_async_remote_copy(
            src_ref=ref,
            dst_ref=ref,
            send_sem=send.at[number],
            recv_sem=recv.at[number],
            device_id=other,
            device_id_type=MESH,
        )
        copy.wait_recv()
        copy.wait_send()

    for a in range(4):
        for b in range(4):
            settle(swap0 + a * 4 + b, x0.at[a, b])
        for b in range(2):
            settle(swap1 + b * 4 + a, x1.at[b, a])
            settle(swap2 + a * 2 + b, x2.at[a, b])

    def select(number, carry):
        y, x, z = number // 8, (number // 2) % 4, number % 2
        zz = 2 * rep + z
        wide = [
            side_by_side(rep, own, came, 1)
            for own, came in (
                (g0[y, x, zz], x0[y, x, z]),
                (g1[zz, y, x], x1[z, y, x]),
                (g2[x, zz, y], x2[x, z, y]),
            )
        ]
        rows = jnp.concatenate([wide[0], wide[1], wide[2][:64]], axis=0)
        slots = dot(ones_at(l3[zz, x, y], 256), rows, 0, 0)
        table[pl.ds(pl.multiple_of(1024 + number * 128, 128), 128)] = slots.astype(jnp.bfloat16)
        table[pl.ds(pl.multiple_of(5120 + number * 32, 32), 32)] = wide[2][64:]
        return carry

    lax.fori_loop(0, 32, select, 0, unroll=8)

    def gather_tile(tile):
        cols = pl.ds(pl.multiple_of(tile * 512, 512), 512)
        value = total[cols]
        for first, some, begin, end in ((8, 4, 1024, 5120), (12, 4, 5120, 6144)):
            chosen = [picks[k : k + 1, cols] for k in range(first, first + some)]
            counts_of = [mult[k : k + 1, cols] for k in range(first, first + some)]
            for base in range(begin, end, 512):
                value = value + dot(
                    one_hot(chosen, counts_of, 512, base - begin), table[base : base + 512], 0, 0
                )
        total[cols] = value

    sums_at = io.used
    io.used += 2

    def sum_copy(k, tile):
        cols = pl.ds(pl.multiple_of(tile * 512, 512), 512)
        return pltpu.make_async_remote_copy(
            src_ref=total.at[cols],
            dst_ref=totalx.at[pl.ds(pl.multiple_of(k * 512, 512), 512)],
            send_sem=send.at[sums_at + k],
            recv_sem=recv.at[sums_at + k],
            device_id=other,
            device_id_type=MESH,
        )

    def gather_theirs(k, carry):
        gather_tile((1 - rep) * 2 + k)
        sum_copy(k, (1 - rep) * 2 + k).start()
        return carry

    def gather_mine(k, carry):
        gather_tile(rep * 2 + k)
        return carry

    lax.fori_loop(0, 2, gather_theirs, 0)
    lax.fori_loop(0, 2, gather_mine, 0)

    selfw = side_by_side(rep, self_weight[...], wsx[...], 0)
    nbrw = side_by_side(rep, neighbor_weight[...], wnx[...], 0)
    grad_ids = [[io.take() for _ in range(3)] for _ in range(2)]
    for step in range(4):
        if step % 2 == 0:
            sum_copy(step // 2, (1 - rep) * 2 + step // 2).wait_recv()
        rows = pl.ds(pl.multiple_of(rep * 1024 + step * 256, 256), 256)
        part = slice(step * 256, step * 256 + 256)
        wide = side_by_side(rep, features[rows], featx[part], 1)
        cotan = side_by_side(rep, cotangent[rows], cotx[part], 1)
        aggregate = ((total[rows] + totalx[part]) * (1.0 / 16.0)).astype(jnp.bfloat16)
        pre_act = dot(wide, selfw) + dot(aggregate, nbrw)
        sigmoid = 1.0 / (1.0 + jnp.exp(-pre_act))
        result = (pre_act * sigmoid).astype(jnp.bfloat16)
        slope = sigmoid * (1.0 + pre_act * (1.0 - sigmoid))
        grad[rows] = (cotan.astype(jnp.float32) * slope).astype(jnp.bfloat16)
        agg_send[part] = jnp.where(rep == 0, aggregate[:, 128:], aggregate[:, :128])
        out_send[part] = jnp.where(rep == 0, result[:, 128:], result[:, :128])
        agg_cols[rows] = jnp.where(rep == 0, aggregate[:, :128], aggregate[:, 128:])
        output[rows] = jnp.where(rep == 0, result[:, :128], result[:, 128:])
        if step % 2 == 1:
            n = grad_ids[step // 2]
            tall = pl.ds(pl.multiple_of(rep * 1024 + (step // 2) * 512, 512), 512)
            flat = pl.ds((step // 2) * 512, 512)
            io.start(n[0], grad.at[tall], grad.at[tall], other)
            io.start(n[1], agg_send.at[flat], agg_cols.at[tall], other)
            io.start(n[2], out_send.at[flat], output.at[tall], other)
    for k in range(2):
        sum_copy(k, (1 - rep) * 2 + k).wait_send()

    own_terms = (
        dot(features[own_rows], grad[own_rows], 0, 0),
        dot(agg_cols[own_rows], grad[own_rows], 0, 0),
    )
    for k in range(2):
        tall = pl.ds(pl.multiple_of((1 - rep) * 1024 + k * 512, 512), 512)
        io.arrived(grad_ids[k][0], grad.at[tall], other)
        io.arrived(grad_ids[k][1], agg_cols.at[tall], other)
    for n, (mine_term, data) in enumerate(zip(own_terms, (features, agg_cols))):
        term = mine_term + dot(data[theirs], grad[theirs], 0, 0)
        for h in range(2):
            for b in range(16):
                terms[2 * n + h, b // 4, b % 4] = term[b * 8 : b * 8 + 8, h * 128 : h * 128 + 128]

    def scatter_step(step, carry):
        sums_of = jnp.zeros((640, 256), jnp.float32)
        for begin in range(0, 2048, 256):
            cols = slice(begin, begin + 256)
            parts = []
            for first, some, rows in ((8, 4, 512), (12, 4, 128)):
                chosen = [picks[k : k + 1, cols] for k in range(first, first + some)]
                counts_of = [mult[k : k + 1, cols] for k in range(first, first + some)]
                parts.append(one_hot(chosen, counts_of, rows, step * rows))
            sums_of = sums_of + dot(jnp.concatenate(parts, axis=0), grad[cols])
        slots = sums_of[0:512].astype(jnp.bfloat16)
        hubs = sums_of[512:640].astype(jnp.bfloat16)
        for k in range(4):
            y, x, z = step // 2, (step % 2) * 2 + k // 2, k % 2
            zz = 2 * rep + z
            rows = dot(ones_at(l3[zz, x, y], 256), slots[k * 128 : k * 128 + 128])
            rows = rows.astype(jnp.bfloat16)
            rows = jnp.concatenate([rows, hubs[k * 32 : k * 32 + 32]], axis=0)
            keep = jnp.where(rep == 0, rows[:, :128], rows[:, 128:])
            give = jnp.where(rep == 0, rows[:, 128:], rows[:, :128])
            parts = [slice(a, a + n) for a, n in zip(SHARE_AT, SHARE)]
            wholes[0][y, x, zz], give0[y, x, z] = keep[parts[0]], give[parts[0]]
            wholes[1][zz, y, x], give1[z, y, x] = keep[parts[1]], give[parts[1]]
            wholes[2][x, zz, y], give2[x, z, y] = keep[parts[2]], give[parts[2]]
        return carry

    def output_done():
        for k in range(2):
            tall = pl.ds(pl.multiple_of((1 - rep) * 1024 + k * 512, 512), 512)
            io.arrived(grad_ids[k][2], output.at[tall], other)

    def trade(axis, src, dst):
        ids = [io.take() for _ in range(3)]
        for delta in (1, 2, 3):
            device = (shifted(dom, at, axis, delta), rep)
            io.start(ids[delta - 1], src(delta), dst(delta), device)
        return ids

    def traded(ids, dst):
        for delta in (1, 2, 3):
            io.arrived(ids[delta - 1], dst(delta), other)

    def reduce_start(axis, src, landing):
        return trade(axis, lambda d: src.at[(at[axis] + d) % 4], lambda d: landing.at[d - 1])

    def reduce_end(ids, src, axis, landing):
        traded(ids, lambda d: landing.at[d - 1])
        return src[at[axis]] + landing[0] + landing[1] + landing[2]

    def give_start(axis, ref):
        return trade(axis, lambda d: ref(at[axis]), lambda d: ref(at[axis]))

    def give_end(ids, axis, ref):
        traded(ids, lambda d: ref((at[axis] - d) % 4))

    gives = {
        "z": lambda j: sums.at[at["y"], at["x"], j],
        "x": lambda j: sums.at[at["y"], j],
        "y": lambda j: sums.at[j],
    }

    swap_ids = [[io.take() for _ in range(4)] for _ in range(3)]

    def swap_refs(chain, piece, half):
        m = (coords[chain][1] + piece) % 4
        span = pl.ds(2 * half, 2)
        if chain == 0:
            return give0.at[:, m], wholes[0].at[:, m, span]
        if chain == 1:
            return give1.at[:, m], wholes[1].at[span, m]
        return give2.at[:, m % 2], wholes[2].at[:, m]

    def remote(number, src, dst):
        return pltpu.make_async_remote_copy(
            src_ref=src,
            dst_ref=dst,
            send_sem=send.at[number],
            recv_sem=recv.at[number],
            device_id=other,
            device_id_type=MESH,
        )

    def swap_start(chain, piece):
        number = swap_ids[chain][piece]
        src, dst = swap_refs(chain, piece, rep)

        def go():
            remote(number, src, dst).start()

        if chain == 2:
            pl.when((coords[2][1] + piece) % 4 // 2 == rep)(go)
        else:
            go()

    def swap_end(chain, piece):
        number = swap_ids[chain][piece]
        src, dst = swap_refs(chain, piece, rep)
        _, came = swap_refs(chain, piece, 1 - rep)

        def kept():
            remote(number, src, dst).wait_send()

        def got():
            remote(number, came, came).wait_recv()

        if chain == 2:
            here = (coords[2][1] + piece) % 4 // 2 == rep
            pl.when(here)(kept)
            pl.when(jnp.logical_not(here))(got)
        else:
            kept()
            got()


    outer_ids = [[[io.take() for _ in range(6)] for _ in range(4)] for _ in range(3)]
    middle_ids = [[io.take() for _ in range(6)] for _ in range(3)]
    inner_ids = [[io.take() for _ in range(3)] for _ in range(3)]
    low2, high2 = pl.ds(0, 2), pl.ds(2, 2)

    def add_into(spot, came):
        spot[...] = (spot[...].astype(jnp.float32) + came[...].astype(jnp.float32)).astype(jnp.bfloat16)

    def three(a, b, c):
        return a[...].astype(jnp.float32) + b[...].astype(jnp.float32) + c[...].astype(jnp.float32)

    def outer_start(piece, chains):
        for chain in chains:
            swap_end(chain, piece)
            o, m, i = coords[chain]
            up, down = ways[chain][0]
            data, m = wholes[chain], (m + piece) % 4
            from_low, from_high, whole_low, whole_high = (r.at[piece] for r in outer_recv[chain])
            n = outer_ids[chain][piece]
            io.start(n[0], data.at[(o + 2) % 4, m, low2], from_low, up)
            io.start(n[1], data.at[(o + 2) % 4, m, high2], from_high, down)
            io.start(n[2], data.at[(o + 1) % 4, m, high2], whole_low.at[high2], up)
            io.start(n[3], data.at[(o + 3) % 4, m, low2], whole_high.at[low2], down)

    def outer_pass(piece, chains):
        for chain in chains:
            o, m, i = coords[chain]
            up, down = ways[chain][0]
            data, m = wholes[chain], (m + piece) % 4
            from_low, from_high, whole_low, whole_high = (r.at[piece] for r in outer_recv[chain])
            n = outer_ids[chain][piece]
            io.arrived(n[0], from_low, other)
            for k in range(2):
                add_into(data.at[(o + 1) % 4, m, k], from_low.at[k])
            io.start(n[4], data.at[(o + 1) % 4, m, low2], whole_low.at[low2], up)
            io.arrived(n[1], from_high, other)
            for k in range(2):
                add_into(data.at[(o + 3) % 4, m, 2 + k], from_high.at[k])
            io.start(n[5], data.at[(o + 3) % 4, m, high2], whole_high.at[high2], down)

    def outer_end(piece, chains):
        for chain in chains:
            o, m, i = coords[chain]
            data, target = wholes[chain], firsts[chain].at[piece]
            _, _, whole_low, whole_high = (r.at[piece] for r in outer_recv[chain])
            n = outer_ids[chain][piece]
            io.arrived(n[2], whole_low.at[high2], other)
            io.arrived(n[3], whole_high.at[low2], other)
            io.arrived(n[4], whole_low.at[low2], other)
            io.arrived(n[5], whole_high.at[high2], other)
            for k in range(4):
                target[k] = three(
                    data.at[o, (m + piece) % 4, k], whole_low.at[k], whole_high.at[k]
                ).astype(jnp.bfloat16)
            up, down = ways[chain][1]
            from_low, from_high, whole_low, whole_high = middle_recv[chain]
            n = middle_ids[chain]
            if piece == 2:
                io.start(n[0], target.at[low2], from_low, up)
                io.start(n[1], target.at[high2], from_high, down)
            if piece == 1:
                io.start(n[2], target.at[high2], whole_low.at[high2], up)
            if piece == 3:
                io.start(n[3], target.at[low2], whole_high.at[low2], down)


    local_ids = [io.take() for _ in range(4)]

    def local_scatter(part):
        value = jnp.zeros((256, 256), jnp.float32)
        for begin in range(0, 2048, 512):
            cols = slice(begin, begin + 512)
            chosen = [picks[k : k + 1, cols] for k in range(8)]
            counts_of = [mult[k : k + 1, cols] for k in range(8)]
            value = value + dot(one_hot(chosen, counts_of, 256, part * 256), grad[cols])
        rows = pl.ds(pl.multiple_of(rep * 1024 + part * 256, 256), 256)
        local_sums[rows] = (value * (1.0 / 16.0)).astype(jnp.bfloat16)
        io.start(local_ids[part], local_sums.at[rows], local_sums.at[rows], other)

    def products(half):
        if half == 0:
            for part in range(4):
                rows = pl.ds(pl.multiple_of((1 - rep) * 1024 + part * 256, 256), 256)
                io.arrived(local_ids[part], local_sums.at[rows], other)
        for begin in range(half * 1024, half * 1024 + 1024, 512):
            rows = slice(begin, begin + 512)
            total[rows, 0:128] = dot(grad[rows], self_weight[...], 1, 1) + dot(
                local_sums[rows], neighbor_weight[...], 1, 1
            )

    def reduce_pass(chains):
        for chain in chains:
            up, down = ways[chain][1]
            from_low, from_high, whole_low, whole_high = middle_recv[chain]
            n = middle_ids[chain]
            io.arrived(n[0], from_low, other)
            for k in range(2):
                add_into(firsts[chain].at[1, k], from_low.at[k])
            io.start(n[4], firsts[chain].at[1, low2], whole_low.at[low2], up)
            io.arrived(n[1], from_high, other)
            for k in range(2):
                add_into(firsts[chain].at[3, 2 + k], from_high.at[k])
            io.start(n[5], firsts[chain].at[3, high2], whole_high.at[high2], down)

    def reduce_last(chains):
        for chain in chains:
            o, m, i = coords[chain]
            from_low, from_high, whole_low, whole_high = middle_recv[chain]
            n = middle_ids[chain]
            io.arrived(n[2], whole_low.at[high2], other)
            io.arrived(n[3], whole_high.at[low2], other)
            io.arrived(n[4], whole_low.at[low2], other)
            io.arrived(n[5], whole_high.at[high2], other)
            target = seconds[chain]
            for k in range(4):
                target[k] = three(
                    firsts[chain].at[0, k], whole_low.at[k], whole_high.at[k]
                ).astype(jnp.bfloat16)
            for delta in (2, 1, 3):
                device = (shifted(dom, at, CHAINS[chain][2], delta), rep)
                io.start(
                    inner_ids[chain][delta - 1],
                    target.at[(i + delta) % 4],
                    inner_recv[chain].at[delta - 1],
                    device,
                )

    def scatter_piece(piece):
        first = 2 * ((at["y"] + piece) % 4)
        lax.fori_loop(0, 2, lambda k, carry: scatter_step(first + k, carry), 0)

    early, late = (1,), (0, 2)
    weigh = reduce_start("y", terms, w1)
    scatter_piece(2)
    swap_start(1, 2)
    scatter_piece(1)
    swap_start(1, 1)
    outer_start(2, early)
    wb[...] = reduce_end(weigh, terms, "y", w1)
    weigh = reduce_start("x", wb, w2)
    scatter_piece(3)
    swap_start(1, 3)
    outer_start(1, early)
    outer_pass(2, early)
    wc[...] = reduce_end(weigh, wb, "x", w2)
    weigh = reduce_start("z", wc, w3)
    scatter_piece(0)
    for piece in (2, 1):
        for chain in late:
            swap_start(chain, piece)
    swap_start(1, 0)
    for piece in (3, 0):
        for chain in late:
            swap_start(chain, piece)
    outer_start(3, early)
    outer_pass(1, early)
    outer_end(2, early)
    outer_start(2, late)
    sums[at["y"], at["x"], at["z"]] = reduce_end(weigh, wc, "z", w3)
    weigh = give_start("z", gives["z"])
    outer_pass(3, early)
    outer_start(1, late)
    outer_end(1, early)
    outer_pass(2, late)
    outer_start(0, early)
    outer_start(3, late)
    outer_end(3, early)
    local_scatter(0)
    outer_pass(1, late)
    outer_end(2, late)
    outer_pass(0, early)
    reduce_pass(early)
    outer_start(0, late)
    local_scatter(1)
    outer_pass(3, late)
    outer_end(1, late)
    give_end(weigh, "z", gives["z"])
    weigh = give_start("x", gives["x"])
    outer_end(0, early)
    reduce_last(early)
    outer_pass(0, late)
    local_scatter(2)
    outer_end(3, late)
    reduce_pass(late)
    local_scatter(3)
    outer_end(0, late)
    give_end(weigh, "x", gives["x"])
    weigh = give_start("y", gives["y"])
    reduce_last(late)
    products(0)
    products(1)
    last = [io.take() for _ in range(3)]
    for chain in (1, 0, 2):
        o, m, i = coords[chain]
        came = inner_recv[chain]
        for delta in (1, 3, 2):
            io.arrived(inner_ids[chain][delta - 1], came.at[delta - 1], other)
        results[chain][rep] = three(seconds[chain].at[i], came.at[0], came.at[2]) + came[1].astype(
            jnp.float32
        )
        io.start(last[chain], results[chain].at[rep], results[chain].at[rep], other)
    give_end(weigh, "y", gives["y"])
    for chain in range(3):
        io.arrived(last[chain], results[chain].at[1 - rep], other)
    output_done()
    tall = jnp.concatenate(
        [jnp.concatenate([r[0], r[1]], axis=1) for r in results], axis=0
    )
    value = dot((tall * (1.0 / 16.0)).astype(jnp.bfloat16), neighbor_weight[...], 1, 1)
    high = value.astype(jnp.bfloat16)
    low = (value - high.astype(jnp.float32)).astype(jnp.bfloat16)
    for begin in range(0, 2048, 512):
        rows = slice(begin, begin + 512)
        gradient[rows] = (
            total[rows, 0:128] + dot(chooser[rows], high) + dot(chooser[rows], low)
        ).astype(jnp.bfloat16)
    for n, target in enumerate((grad_self, grad_neighbor)):
        for h in range(2):
            for b in range(16):
                target[b * 8 : b * 8 + 8, h * 128 : h * 128 + 128] = (
                    sums[2 * n + h, b // 4, b % 4] * NORM
                )
    io.close()


def layer_call(features, cotangent, self_weight, neighbor_weight, raw, brows, hrows, lists, counts):
    args = (features, cotangent, self_weight, neighbor_weight, raw, brows, hrows, lists, counts)
    return pl.pallas_call(
        layer_kernel,
        out_shape=[jax.ShapeDtypeStruct((2048, 128), BF)] * 2
        + [jax.ShapeDtypeStruct((128, 256), F32)] * 2,
        in_specs=[VMEM_SPEC] * 8 + [pl.BlockSpec(memory_space=pltpu.SMEM)],
        out_specs=[VMEM_SPEC] * 4,
        scratch_shapes=[pltpu.VMEM(shape, kind) for _, shape, kind in SCRATCH]
        + [
            pltpu.SemaphoreType.DMA((N_COPIES,)),
            pltpu.SemaphoreType.DMA((N_COPIES,)),
            pltpu.SemaphoreType.DMA((4,)),
        ],
        compiler_params=pltpu.CompilerParams(
            collective_id=0, has_side_effects=True, vmem_limit_bytes=BIG
        ),
        name="layer",
    )(*args)


def hand_over_kernel(*refs):
    for source, target in zip(refs[:4], refs[4:]):
        target[...] = source[...]


def hand_over(*arrays):
    return pl.pallas_call(
        hand_over_kernel,
        out_shape=[jax.ShapeDtypeStruct(a.shape, a.dtype) for a in arrays],
        in_specs=[VMEM_SPEC] * 4,
        out_specs=[VMEM_SPEC] * 4,
        name="hand_over",
    )(*arrays)


def per_device(
    features,
    cotangent,
    self_weight,
    neighbor_weight,
    local_neighbors,
    hub_rows,
    hub_neighbors,
    boundary_rows,
    send_lists,
    received_counts,
    halo_neighbors,
):
    raw = jnp.concatenate([local_neighbors.T, halo_neighbors.T, hub_neighbors.T], axis=0)
    output, gradient, grad_self, grad_neighbor = layer_call(
        features,
        cotangent,
        self_weight,
        neighbor_weight,
        raw,
        boundary_rows[None],
        hub_rows[None],
        send_lists.reshape(4, 4, 4, 1, 128),
        received_counts,
    )
    return tuple(hand_over(output, gradient, grad_self, grad_neighbor))


def solution(mesh):
    return jax.shard_map(
        per_device,
        mesh=mesh,
        in_specs=(
            P("dom", "rep"),
            P("dom", "rep"),
            P("rep", None),
            P("rep", None),
            P("dom", None),
            P("dom"),
            P("dom", None),
            P("dom"),
            P("dom", None, None),
            P("dom", None),
            P("dom", None),
        ),
        out_specs=(P("dom", "rep"), P("dom", "rep"), P("rep", None), P("rep", None)),
        check_vma=False,
    )
```

```python
import functools

import jax
import jax.numpy as jnp
from jax import lax
from jax.experimental import pallas as pl
from jax.experimental.pallas import tpu as pltpu
from jax.sharding import PartitionSpec as P

MESH = pl.DeviceIdType.MESH
VMEM_SPEC = pl.BlockSpec(memory_space=pltpu.VMEM)
STRIDE = {"y": 16, "x": 4, "z": 1}
CHAINS = (("y", "x", "z"), ("z", "y", "x"), ("x", "z", "y"))
UNIT = 96
SHARE = (80, 128, 80)
SHARE_AT = (0, 80, 208)
BIG = 58 * 2**20


def place():
    dom = lax.axis_index("dom")
    rep = lax.axis_index("rep")
    at = {"y": dom // 16, "x": (dom // 4) % 4, "z": dom % 4}
    return dom, rep, at


def shifted(dom, at, axis, delta):
    there = (at[axis] + delta) % 4
    return dom + (there - at[axis]) * STRIDE[axis]


def signal_all(dom, rep, at):
    barrier = pltpu.get_barrier_semaphore()
    for axis in "yxz":
        for delta in (1, 2, 3):
            pl.semaphore_signal(
                barrier, inc=1, device_id=(shifted(dom, at, axis, delta), rep), device_id_type=MESH
            )
    pl.semaphore_signal(barrier, inc=1, device_id=(dom, 1 - rep), device_id_type=MESH)


class Copies:
    def __init__(self, send, recv):
        self.send, self.recv, self.used, self.open = send, recv, 0, []

    def take(self):
        self.used += 1
        return self.used - 1

    def start(self, number, src, dst, device):
        copy = pltpu.make_async_remote_copy(
            src_ref=src,
            dst_ref=dst,
            send_sem=self.send.at[number],
            recv_sem=self.recv.at[number],
            device_id=device,
            device_id_type=MESH,
        )
        copy.start()
        self.open.append(copy)

    def arrived(self, number, dst, device):
        pltpu.make_async_remote_copy(
            src_ref=dst,
            dst_ref=dst,
            send_sem=self.send.at[number],
            recv_sem=self.recv.at[number],
            device_id=device,
            device_id_type=MESH,
        ).wait_recv()

    def close(self):
        for copy in self.open:
            copy.wait_send()
        self.open = []


def one_hot(picks, counts, rows, base):
    nodes = picks[0].shape[1]
    row = lax.broadcasted_iota(jnp.int16, (rows, nodes), 0)
    table = jnp.zeros((rows, nodes), jnp.bfloat16)
    for pick, count in zip(picks, counts):
        here = jnp.broadcast_to(pick - base, (rows, nodes)).astype(jnp.int16)
        table = jnp.where(
            here == row, jnp.broadcast_to(count.astype(jnp.bfloat16), (rows, nodes)), table
        )
    return table


def ones_at(pick, rows, base=0):
    row = lax.broadcasted_iota(jnp.int32, (rows, pick.shape[1]), 0)
    return jnp.where(pick - base == row, 1.0, 0.0).astype(jnp.bfloat16)


def dot(a, b, over_a=1, over_b=0):
    return lax.dot_general(
        a, b, (((over_a,), (over_b,)), ((), ())), preferred_element_type=jnp.float32
    )


def side_by_side(rep, own, other, axis):
    first = jnp.where(rep == 0, own, other)
    second = jnp.where(rep == 0, other, own)
    return jnp.concatenate([first, second], axis=axis)


NORM = 131072.0**-0.5
N_COPIES = 420
PIECES = (0, 3, 1, 2)
ORDER = (2, 1, 3, 0)
BF, F32, I32 = jnp.bfloat16, jnp.float32, jnp.int32
SCRATCH = (
    [("g%d" % c, (4, 4, 4, UNIT, 128), BF) for c in range(3)]
    + [("x0", (4, 4, 2, UNIT, 128), BF), ("x1", (2, 4, 4, UNIT, 128), BF), ("x2", (4, 2, 4, UNIT, 128), BF)]
    + [("give0", (4, 4, 2, SHARE[0], 128), BF), ("give1", (2, 4, 4, SHARE[1], 128), BF)]
    + [("give2", (4, 2, 4, SHARE[2], 128), BF)]
    + [(name, (4, 4, 4, 1, 128), I32) for name in ("l1", "l2", "l3")]
    + [("featx", (1024, 128), BF), ("cotx", (1024, 128), BF), ("wsx", (128, 256), BF), ("wnx", (128, 256), BF)]
    + [("chooser", (2048, 288), BF), ("units", (288, 128), BF)]
    + [("picks", (16, 2048), I32), ("mult", (16, 2048), F32), ("table", (6144, 256), BF)]
    + [("total", (2048, 256), F32), ("totalx", (1024, 256), F32), ("grad", (2048, 256), BF)]
    + [("agg_send", (1024, 128), BF), ("out_send", (1024, 128), BF), ("agg_cols", (2048, 128), BF)]
    + [("terms", (4, 4, 4, 8, 128), F32), ("sums", (4, 4, 4, 8, 128), F32)]
    + [("local_sums", (2048, 256), BF)]
    + [("w1", (3, 4, 4, 8, 128), F32), ("w2", (3, 4, 8, 128), F32), ("wb", (4, 4, 8, 128), F32)]
    + [("wc", (4, 8, 128), F32), ("w3", (3, 8, 128), F32)]
    + [("r%d" % c, (2, SHARE[c], 128), F32) for c in range(3)]
    + [("whole%d" % c, (4, 4, 4, SHARE[c], 128), BF) for c in range(3)]
    + [("first%d" % c, (4, 4, SHARE[c], 128), BF) for c in range(3)]
    + [("second%d" % c, (4, SHARE[c], 128), BF) for c in range(3)]
    + [("inner%d" % c, (3, SHARE[c], 128), BF) for c in range(3)]
    + [
        ("%s%d%d" % (stage, c, n), lead + (2 if n < 2 else 4, SHARE[c], 128), BF)
        for stage, lead in (("outer", (4,)), ("middle", ()))
        for c in range(3)
        for n in range(4)
    ]
)


def layer_kernel(*refs):
    features, cotangent, self_weight, neighbor_weight, local_in, halo_in, hub_in = refs[:7]
    brows, hrows, lists, counts = refs[7:11]
    output, gradient, grad_self, grad_neighbor = refs[11:15]
    named = {name: ref for (name, _, _), ref in zip(SCRATCH, refs[15:])}
    send, recv, local = refs[15 + len(SCRATCH) :]
    g0, g1, g2 = bufs = [named["g%d" % c] for c in range(3)]
    x0, x1, x2 = [named["x%d" % c] for c in range(3)]
    give0, give1, give2 = [named["give%d" % c] for c in range(3)]
    l1, l2, l3 = named["l1"], named["l2"], named["l3"]
    featx, cotx, wsx, wnx = named["featx"], named["cotx"], named["wsx"], named["wnx"]
    chooser, units, picks, mult = named["chooser"], named["units"], named["picks"], named["mult"]
    table, total, totalx, grad = named["table"], named["total"], named["totalx"], named["grad"]
    agg_send, out_send, agg_cols = named["agg_send"], named["out_send"], named["agg_cols"]
    terms, sums, local_sums = named["terms"], named["sums"], named["local_sums"]
    w1, w2, wb, wc, w3 = (named[name] for name in ("w1", "w2", "wb", "wc", "w3"))
    results = [named["r%d" % c] for c in range(3)]
    wholes = [named["whole%d" % c] for c in range(3)]
    firsts = [named["first%d" % c] for c in range(3)]
    seconds = [named["second%d" % c] for c in range(3)]
    outer_recv, middle_recv = (
        [[named["%s%d%d" % (stage, c, n)] for n in range(4)] for c in range(3)]
        for stage in ("outer", "middle")
    )
    inner_recv = [named["inner%d" % c] for c in range(3)]
    dom, rep, at = place()
    other = (dom, 1 - rep)
    io = Copies(send, recv)
    signal_all(dom, rep, at)
    chooser[:, 0:256] = ones_at(brows[...], 2048)
    chooser[:, 256:288] = ones_at(hrows[...], 2048)
    units[...] = dot(chooser[...], features[...], 0, 0).astype(BF)
    pl.semaphore_wait(pltpu.get_barrier_semaphore(), 10)

    def prepare():
        halo = halo_in[...]
        end = jnp.int32(0)
        sender = jnp.zeros_like(halo)
        before = jnp.zeros_like(halo)
        for p in range(64):
            end = end + counts[0, p]
            passed = halo >= end
            sender = sender + jnp.where(passed, 1, 0)
            before = before + jnp.where(passed, counts[0, p], 0)
        sender = jnp.minimum(sender, 63)
        slot = jnp.clip(halo - before, 0, 127)

        def in_half(p, within, size):
            number = (p >> 2) * 2 + (p & 1)
            return jnp.where(((p & 3) >> 1) == rep, number * size + within, -1)

        hub = hub_in[...]
        local = local_in[...] - rep * 1024
        local = jnp.where((local >= 0) & (local < 1024), local, -1)
        groups = (local, in_half(sender, slot, 128), in_half(hub >> 5, hub & 31, 32))
        start = 0
        for group in groups:
            size = group.shape[0]
            picks[start : start + size] = group
            for a in range(size):
                total = jnp.zeros((1, group.shape[1]), jnp.float32)
                for b in range(size):
                    total = total + jnp.where(group[a : a + 1] == group[b : b + 1], 1.0, 0.0)
                mult[start + a : start + a + 1] = total
            start += size

    def local_gather(tile):
        cols = slice(tile * 512, tile * 512 + 512)
        chosen = [picks[k : k + 1, cols] for k in range(8)]
        counts_of = [mult[k : k + 1, cols] for k in range(8)]
        total[cols] = dot(one_hot(chosen, counts_of, 512, 0), table[0:512], 0, 0) + dot(
            one_hot(chosen, counts_of, 512, 512), table[512:1024], 0, 0
        )

    coords = [tuple(at[a] for a in CHAINS[chain]) for chain in range(3)]
    ways = [
        [
            ((shifted(dom, at, a, 1), rep), (shifted(dom, at, a, 3), rep))
            for a in CHAINS[chain]
        ]
        for chain in range(3)
    ]

    inner_ids = [[io.take() for _ in range(3)] for _ in range(3)]
    mine = []
    for chain in range(3):
        o, m, i = coords[chain]
        unit = units.at[pl.ds(chain * UNIT, UNIT)]
        for delta in (1, 3, 2):
            device = (shifted(dom, at, CHAINS[chain][2], delta), rep)
            io.start(inner_ids[chain][delta - 1], unit, bufs[chain].at[o, m, i], device)
        copy = pltpu.make_async_copy(unit, bufs[chain].at[o, m, i], local.at[chain])
        copy.start()
        mine.append(copy)

    list_steps = (
        ("y", lambda j: lists.at[j], lambda j: l1.at[j]),
        ("x", lambda j: l1.at[:, j], lambda j: l2.at[j]),
        ("z", lambda j: l2.at[:, :, j], lambda j: l3.at[j]),
    )
    list_ids = [[io.take() for _ in range(3)] for _ in range(3)]

    def send_lists(step):
        axis, src, dst = list_steps[step]
        for delta in (1, 2, 3):
            there = (at[axis] + delta) % 4
            io.start(
                list_ids[step][delta - 1],
                src(there),
                dst(at[axis]),
                (shifted(dom, at, axis, delta), rep),
            )
        copy = pltpu.make_async_copy(src(at[axis]), dst(at[axis]), local.at[3])
        copy.start()
        return copy

    def take_lists(step, copy):
        axis, _, dst = list_steps[step]
        copy.wait()
        for delta in (1, 2, 3):
            io.arrived(list_ids[step][delta - 1], dst((at[axis] - delta) % 4), other)

    theirs = pl.ds(pl.multiple_of((1 - rep) * 1024, 1024), 1024)
    pairs = (
        (features.at[theirs], featx),
        (self_weight, wsx),
        (neighbor_weight, wnx),
        (cotangent.at[theirs], cotx),
    )
    pair_ids = [io.take() for _ in pairs]
    for number, (src, dst) in zip(pair_ids, pairs):
        io.start(number, src, dst, other)
    listed = send_lists(0)

    swap0, swap1, swap2 = io.used, io.used + 16, io.used + 24
    io.used += 32

    def swap(chain, o, m):
        if chain == 0:
            pltpu.make_async_remote_copy(
                src_ref=g0.at[o, m, pl.ds(2 * (1 - rep), 2)],
                dst_ref=x0.at[o, m],
                send_sem=send.at[swap0 + o * 4 + m],
                recv_sem=recv.at[swap0 + o * 4 + m],
                device_id=other,
                device_id_type=MESH,
            ).start()
            return
        z = o if chain == 1 else m

        @pl.when(z // 2 != rep)
        def _():
            if chain == 1:
                number, dst = swap1 + (o % 2) * 4 + m, x1.at[o % 2, m]
            else:
                number, dst = swap2 + o * 2 + m % 2, x2.at[o, m % 2]
            pltpu.make_async_remote_copy(
                src_ref=bufs[chain].at[o, m],
                dst_ref=dst,
                send_sem=send.at[number],
                recv_sem=recv.at[number],
                device_id=other,
                device_id_type=MESH,
            ).start()

    middle_ids = [[io.take() for _ in range(4)] for _ in range(3)]
    outer_ids = [[[io.take() for _ in range(4)] for _ in range(4)] for _ in range(3)]

    def spread(chain, piece):
        o, m, _ = coords[chain]
        up, down = ways[chain][0]
        block = bufs[chain].at[o, (m + piece) % 4]
        ids = outer_ids[chain][piece]
        io.start(ids[0], block, block, up)
        io.start(ids[1], block, block, down)
        swap(chain, o, (m + piece) % 4)

    def pass_on(chain, ids, from_down, from_up, half, up, down):
        io.arrived(ids[0], from_down, down)
        io.start(ids[2], half(from_down, 0), half(from_down, 0), up)
        io.arrived(ids[1], from_up, up)
        io.start(ids[3], half(from_up, 1), half(from_up, 1), down)

    def units_half(ref, which):
        return ref.at[pl.ds(which * 2, 2)]


    def inner_end():
        for chain in range(3):
            o, m, i = coords[chain]
            mine[chain].wait()
            for delta in (1, 3, 2):
                io.arrived(inner_ids[chain][delta - 1], bufs[chain].at[o, m, (i - delta) % 4], other)
            up, down = ways[chain][1]
            block = bufs[chain].at[o, m]
            io.start(middle_ids[chain][0], block, block, up)
            io.start(middle_ids[chain][1], block, block, down)
            spread(chain, 0)

    def middle_pass():
        for chain in range(3):
            o, m, i = coords[chain]
            up, down = ways[chain][1]
            buf = bufs[chain]
            pass_on(
                chain,
                middle_ids[chain],
                buf.at[o, (m + 3) % 4],
                buf.at[o, (m + 1) % 4],
                units_half,
                up,
                down,
            )
            spread(chain, 3)
            spread(chain, 1)

    def middle_end():
        for chain in range(3):
            o, m, i = coords[chain]
            up, down = ways[chain][1]
            far = bufs[chain].at[o, (m + 2) % 4]
            io.arrived(middle_ids[chain][2], units_half(far, 0), down)
            io.arrived(middle_ids[chain][3], units_half(far, 1), up)
            spread(chain, 2)

    def spread_pass(piece):
        for chain in range(3):
            o, m, i = coords[chain]
            up, down = ways[chain][0]
            buf, at_m = bufs[chain], (m + piece) % 4
            pass_on(
                chain,
                outer_ids[chain][piece],
                buf.at[(o + 3) % 4, at_m],
                buf.at[(o + 1) % 4, at_m],
                units_half,
                up,
                down,
            )
            swap(chain, (o + 3) % 4, at_m)
            swap(chain, (o + 1) % 4, at_m)

    def spread_end(piece):
        for chain in range(3):
            o, m, i = coords[chain]
            up, down = ways[chain][0]
            far = bufs[chain].at[(o + 2) % 4, (m + piece) % 4]
            io.arrived(outer_ids[chain][piece][2], units_half(far, 0), down)
            io.arrived(outer_ids[chain][piece][3], units_half(far, 1), up)
            swap(chain, (o + 2) % 4, (m + piece) % 4)

    inner_end()
    prepare()
    take_lists(0, listed)
    listed = send_lists(1)
    for number, (_, dst) in zip(pair_ids, pairs):
        io.arrived(number, dst, other)
    own_rows = pl.ds(pl.multiple_of(rep * 1024, 1024), 1024)
    table[0:1024] = side_by_side(rep, features[own_rows], featx[...], 1)
    middle_pass()
    take_lists(1, listed)
    listed = send_lists(2)
    spread_pass(0)
    middle_end()
    local_gather(0)
    spread_end(0)
    spread_pass(3)
    local_gather(1)
    spread_pass(1)
    local_gather(2)
    spread_end(3)
    spread_pass(2)
    local_gather(3)
    take_lists(2, listed)
    spread_end(1)
    spread_end(2)

    def settle(number, ref):
        copy = pltpu.make_async_remote_copy(
            src_ref=ref,
            dst_ref=ref,
            send_sem=send.at[number],
            recv_sem=recv.at[number],
            device_id=other,
            device_id_type=MESH,
        )
        copy.wait_recv()
        copy.wait_send()

    for a in range(4):
        for b in range(4):
            settle(swap0 + a * 4 + b, x0.at[a, b])
        for b in range(2):
            settle(swap1 + b * 4 + a, x1.at[b, a])
            settle(swap2 + a * 2 + b, x2.at[a, b])

    def select(number, carry):
        y, x, z = number // 8, (number // 2) % 4, number % 2
        zz = 2 * rep + z
        wide = [
            side_by_side(rep, own, came, 1)
            for own, came in (
                (g0[y, x, zz], x0[y, x, z]),
                (g1[zz, y, x], x1[z, y, x]),
                (g2[x, zz, y], x2[x, z, y]),
            )
        ]
        rows = jnp.concatenate([wide[0], wide[1], wide[2][:64]], axis=0)
        slots = dot(ones_at(l3[zz, x, y], 256), rows, 0, 0)
        table[pl.ds(pl.multiple_of(1024 + number * 128, 128), 128)] = slots.astype(jnp.bfloat16)
        table[pl.ds(pl.multiple_of(5120 + number * 32, 32), 32)] = wide[2][64:]
        return carry

    lax.fori_loop(0, 32, select, 0, unroll=16)

    def gather_tile(tile):
        cols = pl.ds(pl.multiple_of(tile * 512, 512), 512)
        value = total[cols]
        for first, some, begin, end in ((8, 4, 1024, 5120), (12, 4, 5120, 6144)):
            chosen = [picks[k : k + 1, cols] for k in range(first, first + some)]
            counts_of = [mult[k : k + 1, cols] for k in range(first, first + some)]
            for base in range(begin, end, 512):
                value = value + dot(
                    one_hot(chosen, counts_of, 512, base - begin), table[base : base + 512], 0, 0
                )
        total[cols] = value

    sums_at = io.used
    io.used += 2

    def sum_copy(k, tile):
        cols = pl.ds(pl.multiple_of(tile * 512, 512), 512)
        return pltpu.make_async_remote_copy(
            src_ref=total.at[cols],
            dst_ref=totalx.at[pl.ds(pl.multiple_of(k * 512, 512), 512)],
            send_sem=send.at[sums_at + k],
            recv_sem=recv.at[sums_at + k],
            device_id=other,
            device_id_type=MESH,
        )

    def gather_theirs(k, carry):
        gather_tile((1 - rep) * 2 + k)
        sum_copy(k, (1 - rep) * 2 + k).start()
        return carry

    def gather_mine(k, carry):
        gather_tile(rep * 2 + k)
        return carry

    lax.fori_loop(0, 2, gather_theirs, 0)
    lax.fori_loop(0, 2, gather_mine, 0)

    selfw = side_by_side(rep, self_weight[...], wsx[...], 0)
    nbrw = side_by_side(rep, neighbor_weight[...], wnx[...], 0)
    grad_ids = [[io.take() for _ in range(3)] for _ in range(2)]
    for step in range(4):
        if step % 2 == 0:
            sum_copy(step // 2, (1 - rep) * 2 + step // 2).wait_recv()
        rows = pl.ds(pl.multiple_of(rep * 1024 + step * 256, 256), 256)
        part = slice(step * 256, step * 256 + 256)
        wide = side_by_side(rep, features[rows], featx[part], 1)
        cotan = side_by_side(rep, cotangent[rows], cotx[part], 1)
        aggregate = ((total[rows] + totalx[part]) * (1.0 / 16.0)).astype(jnp.bfloat16)
        pre_act = dot(wide, selfw) + dot(aggregate, nbrw)
        sigmoid = 1.0 / (1.0 + jnp.exp(-pre_act))
        result = (pre_act * sigmoid).astype(jnp.bfloat16)
        slope = sigmoid * (1.0 + pre_act * (1.0 - sigmoid))
        grad[rows] = (cotan.astype(jnp.float32) * slope).astype(jnp.bfloat16)
        agg_send[part] = jnp.where(rep == 0, aggregate[:, 128:], aggregate[:, :128])
        out_send[part] = jnp.where(rep == 0, result[:, 128:], result[:, :128])
        agg_cols[rows] = jnp.where(rep == 0, aggregate[:, :128], aggregate[:, 128:])
        output[rows] = jnp.where(rep == 0, result[:, :128], result[:, 128:])
        if step % 2 == 1:
            n = grad_ids[step // 2]
            tall = pl.ds(pl.multiple_of(rep * 1024 + (step // 2) * 512, 512), 512)
            flat = pl.ds((step // 2) * 512, 512)
            io.start(n[0], grad.at[tall], grad.at[tall], other)
            io.start(n[1], agg_send.at[flat], agg_cols.at[tall], other)
            io.start(n[2], out_send.at[flat], output.at[tall], other)
    for k in range(2):
        sum_copy(k, (1 - rep) * 2 + k).wait_send()

    own_terms = (
        dot(features[own_rows], grad[own_rows], 0, 0),
        dot(agg_cols[own_rows], grad[own_rows], 0, 0),
    )
    for k in range(2):
        tall = pl.ds(pl.multiple_of((1 - rep) * 1024 + k * 512, 512), 512)
        io.arrived(grad_ids[k][0], grad.at[tall], other)
        io.arrived(grad_ids[k][1], agg_cols.at[tall], other)

    def finish_terms():
        for n, (mine_term, data) in enumerate(zip(own_terms, (features, agg_cols))):
            term = mine_term + dot(data[theirs], grad[theirs], 0, 0)
            for h in range(2):
                for b in range(16):
                    terms[2 * n + h, b // 4, b % 4] = term[b * 8 : b * 8 + 8, h * 128 : h * 128 + 128]

    def scatter_step(step, carry):
        sums_of = jnp.zeros((640, 256), jnp.float32)
        for begin in range(0, 2048, 256):
            cols = slice(begin, begin + 256)
            parts = []
            for first, some, rows in ((8, 4, 512), (12, 4, 128)):
                chosen = [picks[k : k + 1, cols] for k in range(first, first + some)]
                counts_of = [mult[k : k + 1, cols] for k in range(first, first + some)]
                parts.append(one_hot(chosen, counts_of, rows, step * rows))
            sums_of = sums_of + dot(jnp.concatenate(parts, axis=0), grad[cols])
        slots = sums_of[0:512].astype(jnp.bfloat16)
        hubs = sums_of[512:640].astype(jnp.bfloat16)
        for k in range(4):
            y, x, z = step // 2, (step % 2) * 2 + k // 2, k % 2
            zz = 2 * rep + z
            rows = dot(ones_at(l3[zz, x, y], 256), slots[k * 128 : k * 128 + 128])
            rows = rows.astype(jnp.bfloat16)
            rows = jnp.concatenate([rows, hubs[k * 32 : k * 32 + 32]], axis=0)
            keep = jnp.where(rep == 0, rows[:, :128], rows[:, 128:])
            give = jnp.where(rep == 0, rows[:, 128:], rows[:, :128])
            parts = [slice(a, a + n) for a, n in zip(SHARE_AT, SHARE)]
            wholes[0][y, x, zz], give0[y, x, z] = keep[parts[0]], give[parts[0]]
            wholes[1][zz, y, x], give1[z, y, x] = keep[parts[1]], give[parts[1]]
            wholes[2][x, zz, y], give2[x, z, y] = keep[parts[2]], give[parts[2]]
        return carry

    def output_done():
        for k in range(2):
            tall = pl.ds(pl.multiple_of((1 - rep) * 1024 + k * 512, 512), 512)
            io.arrived(grad_ids[k][2], output.at[tall], other)

    def trade(axis, src, dst):
        ids = [io.take() for _ in range(3)]
        for delta in (1, 2, 3):
            device = (shifted(dom, at, axis, delta), rep)
            io.start(ids[delta - 1], src(delta), dst(delta), device)
        return ids

    def traded(ids, dst):
        for delta in (1, 2, 3):
            io.arrived(ids[delta - 1], dst(delta), other)

    def reduce_start(axis, src, landing):
        return trade(axis, lambda d: src.at[(at[axis] + d) % 4], lambda d: landing.at[d - 1])

    def reduce_end(ids, src, axis, landing):
        traded(ids, lambda d: landing.at[d - 1])
        return src[at[axis]] + landing[0] + landing[1] + landing[2]

    def give_start(axis, ref):
        return trade(axis, lambda d: ref(at[axis]), lambda d: ref(at[axis]))

    def give_end(ids, axis, ref):
        traded(ids, lambda d: ref((at[axis] - d) % 4))

    gives = {
        "z": lambda j: sums.at[at["y"], at["x"], j],
        "x": lambda j: sums.at[at["y"], j],
        "y": lambda j: sums.at[j],
    }

    swap_ids = [[io.take() for _ in range(4)] for _ in range(3)]

    def swap_refs(chain, piece, half):
        m = (coords[chain][1] + piece) % 4
        span = pl.ds(2 * half, 2)
        if chain == 0:
            return give0.at[:, m], wholes[0].at[:, m, span]
        if chain == 1:
            return give1.at[:, m], wholes[1].at[span, m]
        return give2.at[:, m % 2], wholes[2].at[:, m]

    def remote(number, src, dst):
        return pltpu.make_async_remote_copy(
            src_ref=src,
            dst_ref=dst,
            send_sem=send.at[number],
            recv_sem=recv.at[number],
            device_id=other,
            device_id_type=MESH,
        )

    def swap_start(chain, piece):
        number = swap_ids[chain][piece]
        src, dst = swap_refs(chain, piece, rep)

        def go():
            remote(number, src, dst).start()

        if chain == 2:
            pl.when((coords[2][1] + piece) % 4 // 2 == rep)(go)
        else:
            go()

    def swap_end(chain, piece):
        number = swap_ids[chain][piece]
        src, dst = swap_refs(chain, piece, rep)
        _, came = swap_refs(chain, piece, 1 - rep)

        def kept():
            remote(number, src, dst).wait_send()

        def got():
            remote(number, came, came).wait_recv()

        if chain == 2:
            here = (coords[2][1] + piece) % 4 // 2 == rep
            pl.when(here)(kept)
            pl.when(jnp.logical_not(here))(got)
        else:
            kept()
            got()


    outer_ids = [[[io.take() for _ in range(6)] for _ in range(4)] for _ in range(3)]
    middle_ids = [[io.take() for _ in range(6)] for _ in range(3)]
    inner_ids = [[io.take() for _ in range(3)] for _ in range(3)]
    low2, high2 = pl.ds(0, 2), pl.ds(2, 2)

    def add_into(spot, came):
        spot[...] = (spot[...].astype(jnp.float32) + came[...].astype(jnp.float32)).astype(jnp.bfloat16)

    def three(a, b, c):
        return a[...].astype(jnp.float32) + b[...].astype(jnp.float32) + c[...].astype(jnp.float32)

    def outer_start(piece, chains):
        for chain in chains:
            swap_end(chain, piece)
            o, m, i = coords[chain]
            up, down = ways[chain][0]
            data, m = wholes[chain], (m + piece) % 4
            from_low, from_high, whole_low, whole_high = (r.at[piece] for r in outer_recv[chain])
            n = outer_ids[chain][piece]
            io.start(n[0], data.at[(o + 2) % 4, m, low2], from_low, up)
            io.start(n[1], data.at[(o + 2) % 4, m, high2], from_high, down)
            io.start(n[2], data.at[(o + 1) % 4, m, high2], whole_low.at[high2], up)
            io.start(n[3], data.at[(o + 3) % 4, m, low2], whole_high.at[low2], down)

    def outer_pass(piece, chains):
        for chain in chains:
            o, m, i = coords[chain]
            up, down = ways[chain][0]
            data, m = wholes[chain], (m + piece) % 4
            from_low, from_high, whole_low, whole_high = (r.at[piece] for r in outer_recv[chain])
            n = outer_ids[chain][piece]
            io.arrived(n[0], from_low, other)
            for k in range(2):
                add_into(data.at[(o + 1) % 4, m, k], from_low.at[k])
            io.start(n[4], data.at[(o + 1) % 4, m, low2], whole_low.at[low2], up)
            io.arrived(n[1], from_high, other)
            for k in range(2):
                add_into(data.at[(o + 3) % 4, m, 2 + k], from_high.at[k])
            io.start(n[5], data.at[(o + 3) % 4, m, high2], whole_high.at[high2], down)

    def outer_end(piece, chains):
        for chain in chains:
            o, m, i = coords[chain]
            data, target = wholes[chain], firsts[chain].at[piece]
            _, _, whole_low, whole_high = (r.at[piece] for r in outer_recv[chain])
            n = outer_ids[chain][piece]
            io.arrived(n[2], whole_low.at[high2], other)
            io.arrived(n[3], whole_high.at[low2], other)
            io.arrived(n[4], whole_low.at[low2], other)
            io.arrived(n[5], whole_high.at[high2], other)
            for k in range(4):
                target[k] = three(
                    data.at[o, (m + piece) % 4, k], whole_low.at[k], whole_high.at[k]
                ).astype(jnp.bfloat16)
            up, down = ways[chain][1]
            from_low, from_high, whole_low, whole_high = middle_recv[chain]
            n = middle_ids[chain]
            if piece == 2:
                io.start(n[0], target.at[low2], from_low, up)
                io.start(n[1], target.at[high2], from_high, down)
            if piece == 1:
                io.start(n[2], target.at[high2], whole_low.at[high2], up)
            if piece == 3:
                io.start(n[3], target.at[low2], whole_high.at[low2], down)


    local_ids = [io.take() for _ in range(4)]

    def local_scatter(part):
        value = jnp.zeros((256, 256), jnp.float32)
        for begin in range(0, 2048, 512):
            cols = slice(begin, begin + 512)
            chosen = [picks[k : k + 1, cols] for k in range(8)]
            counts_of = [mult[k : k + 1, cols] for k in range(8)]
            value = value + dot(one_hot(chosen, counts_of, 256, part * 256), grad[cols])
        rows = pl.ds(pl.multiple_of(rep * 1024 + part * 256, 256), 256)
        local_sums[rows] = (value * (1.0 / 16.0)).astype(jnp.bfloat16)
        io.start(local_ids[part], local_sums.at[rows], local_sums.at[rows], other)

    def products(half):
        if half == 0:
            for part in range(4):
                rows = pl.ds(pl.multiple_of((1 - rep) * 1024 + part * 256, 256), 256)
                io.arrived(local_ids[part], local_sums.at[rows], other)
        for begin in range(half * 1024, half * 1024 + 1024, 512):
            rows = slice(begin, begin + 512)
            total[rows, 0:128] = dot(grad[rows], self_weight[...], 1, 1) + dot(
                local_sums[rows], neighbor_weight[...], 1, 1
            )

    def reduce_pass(chains):
        for chain in chains:
            up, down = ways[chain][1]
            from_low, from_high, whole_low, whole_high = middle_recv[chain]
            n = middle_ids[chain]
            io.arrived(n[0], from_low, other)
            for k in range(2):
                add_into(firsts[chain].at[1, k], from_low.at[k])
            io.start(n[4], firsts[chain].at[1, low2], whole_low.at[low2], up)
            io.arrived(n[1], from_high, other)
            for k in range(2):
                add_into(firsts[chain].at[3, 2 + k], from_high.at[k])
            io.start(n[5], firsts[chain].at[3, high2], whole_high.at[high2], down)

    def reduce_last(chains):
        for chain in chains:
            o, m, i = coords[chain]
            from_low, from_high, whole_low, whole_high = middle_recv[chain]
            n = middle_ids[chain]
            io.arrived(n[2], whole_low.at[high2], other)
            io.arrived(n[3], whole_high.at[low2], other)
            io.arrived(n[4], whole_low.at[low2], other)
            io.arrived(n[5], whole_high.at[high2], other)
            target = seconds[chain]
            for k in range(4):
                target[k] = three(
                    firsts[chain].at[0, k], whole_low.at[k], whole_high.at[k]
                ).astype(jnp.bfloat16)
            for delta in (2, 1, 3):
                device = (shifted(dom, at, CHAINS[chain][2], delta), rep)
                io.start(
                    inner_ids[chain][delta - 1],
                    target.at[(i + delta) % 4],
                    inner_recv[chain].at[delta - 1],
                    device,
                )

    def scatter_piece(piece):
        first = 2 * ((at["y"] + piece) % 4)
        lax.fori_loop(0, 2, lambda k, carry: scatter_step(first + k, carry), 0)

    early, late = (1,), (0, 2)
    scatter_piece(2)
    swap_start(1, 2)
    scatter_piece(1)
    swap_start(1, 1)
    outer_start(2, early)
    scatter_piece(3)
    swap_start(1, 3)
    outer_start(1, early)
    outer_pass(2, early)
    scatter_piece(0)
    for piece in (2, 1):
        for chain in late:
            swap_start(chain, piece)
    swap_start(1, 0)
    for piece in (3, 0):
        for chain in late:
            swap_start(chain, piece)
    finish_terms()
    weigh = reduce_start("y", terms, w1)
    outer_start(3, early)
    outer_pass(1, early)
    outer_end(2, early)
    outer_start(2, late)
    local_scatter(0)
    wb[...] = reduce_end(weigh, terms, "y", w1)
    weigh = reduce_start("x", wb, w2)
    outer_pass(3, early)
    outer_start(1, late)
    outer_end(1, early)
    outer_pass(2, late)
    outer_start(0, early)
    outer_start(3, late)
    wc[...] = reduce_end(weigh, wb, "x", w2)
    weigh = reduce_start("z", wc, w3)
    outer_end(3, early)
    local_scatter(1)
    outer_pass(1, late)
    outer_end(2, late)
    sums[at["y"], at["x"], at["z"]] = reduce_end(weigh, wc, "z", w3)
    weigh = give_start("z", gives["z"])
    outer_pass(0, early)
    reduce_pass(early)
    outer_start(0, late)
    local_scatter(2)
    outer_pass(3, late)
    outer_end(1, late)
    give_end(weigh, "z", gives["z"])
    weigh = give_start("x", gives["x"])
    outer_end(0, early)
    reduce_last(early)
    outer_pass(0, late)
    local_scatter(3)
    outer_end(3, late)
    reduce_pass(late)
    outer_end(0, late)
    reduce_last(late)
    give_end(weigh, "x", gives["x"])
    weigh = give_start("y", gives["y"])
    products(0)
    products(1)
    last = [io.take() for _ in range(3)]
    for chain in (1, 0, 2):
        o, m, i = coords[chain]
        came = inner_recv[chain]
        for delta in (1, 3, 2):
            io.arrived(inner_ids[chain][delta - 1], came.at[delta - 1], other)
        results[chain][rep] = three(seconds[chain].at[i], came.at[0], came.at[2]) + came[1].astype(
            jnp.float32
        )
        io.start(last[chain], results[chain].at[rep], results[chain].at[rep], other)
    give_end(weigh, "y", gives["y"])
    for chain in range(3):
        io.arrived(last[chain], results[chain].at[1 - rep], other)
    output_done()
    tall = jnp.concatenate(
        [jnp.concatenate([r[0], r[1]], axis=1) for r in results], axis=0
    )
    value = dot((tall * (1.0 / 16.0)).astype(jnp.bfloat16), neighbor_weight[...], 1, 1)
    high = value.astype(jnp.bfloat16)
    low = (value - high.astype(jnp.float32)).astype(jnp.bfloat16)
    pieces = jnp.concatenate([high, low], axis=1)
    for begin in range(0, 2048, 512):
        rows = slice(begin, begin + 512)
        both = dot(chooser[rows], pieces)
        gradient[rows] = (
            total[rows, 0:128] + both[:, 0:128] + both[:, 128:256]
        ).astype(jnp.bfloat16)
    for n, target in enumerate((grad_self, grad_neighbor)):
        for h in range(2):
            for b in range(16):
                target[b * 8 : b * 8 + 8, h * 128 : h * 128 + 128] = (
                    sums[2 * n + h, b // 4, b % 4] * NORM
                )
    io.close()


def layer_call(*args):
    return pl.pallas_call(
        layer_kernel,
        out_shape=[jax.ShapeDtypeStruct((2048, 128), BF)] * 2
        + [jax.ShapeDtypeStruct((128, 256), F32)] * 2,
        in_specs=[VMEM_SPEC] * 10 + [pl.BlockSpec(memory_space=pltpu.SMEM)],
        out_specs=[VMEM_SPEC] * 4,
        scratch_shapes=[pltpu.VMEM(shape, kind) for _, shape, kind in SCRATCH]
        + [
            pltpu.SemaphoreType.DMA((N_COPIES,)),
            pltpu.SemaphoreType.DMA((N_COPIES,)),
            pltpu.SemaphoreType.DMA((4,)),
        ],
        compiler_params=pltpu.CompilerParams(
            collective_id=0, has_side_effects=True, vmem_limit_bytes=BIG
        ),
        name="layer",
    )(*args)


def hand_over_kernel(*refs):
    for source, target in zip(refs[:4], refs[4:]):
        target[...] = source[...]


def hand_over(*arrays):
    return pl.pallas_call(
        hand_over_kernel,
        out_shape=[jax.ShapeDtypeStruct(a.shape, a.dtype) for a in arrays],
        in_specs=[VMEM_SPEC] * 4,
        out_specs=[VMEM_SPEC] * 4,
        name="hand_over",
    )(*arrays)


def per_device(
    features,
    cotangent,
    self_weight,
    neighbor_weight,
    local_neighbors,
    hub_rows,
    hub_neighbors,
    boundary_rows,
    send_lists,
    received_counts,
    halo_neighbors,
):
    output, gradient, grad_self, grad_neighbor = layer_call(
        features,
        cotangent,
        self_weight,
        neighbor_weight,
        local_neighbors.T,
        halo_neighbors.T,
        hub_neighbors.T,
        boundary_rows[None],
        hub_rows[None],
        send_lists.reshape(4, 4, 4, 1, 128),
        received_counts,
    )
    return tuple(hand_over(output, gradient, grad_self, grad_neighbor))


def solution(mesh):
    return jax.shard_map(
        per_device,
        mesh=mesh,
        in_specs=(
            P("dom", "rep"),
            P("dom", "rep"),
            P("rep", None),
            P("rep", None),
            P("dom", None),
            P("dom"),
            P("dom", None),
            P("dom"),
            P("dom", None, None),
            P("dom", None),
            P("dom", None),
        ),
        out_specs=(P("dom", "rep"), P("dom", "rep"), P("rep", None), P("rep", None)),
        check_vma=False,
    )
```

```python
import functools

import jax
import jax.numpy as jnp
from jax import lax
from jax.experimental import pallas as pl
from jax.experimental.pallas import tpu as pltpu
from jax.sharding import PartitionSpec as P

MESH = pl.DeviceIdType.MESH
VMEM_SPEC = pl.BlockSpec(memory_space=pltpu.VMEM)
STRIDE = {"y": 16, "x": 4, "z": 1}
CHAINS = (("y", "x", "z"), ("z", "y", "x"), ("x", "z", "y"))
UNIT = 96
SHARE = (80, 128, 80)
SHARE_AT = (0, 80, 208)
BIG = 58 * 2**20


def place():
    dom = lax.axis_index("dom")
    rep = lax.axis_index("rep")
    at = {"y": dom // 16, "x": (dom // 4) % 4, "z": dom % 4}
    return dom, rep, at


def shifted(dom, at, axis, delta):
    there = (at[axis] + delta) % 4
    return dom + (there - at[axis]) * STRIDE[axis]


def signal_all(dom, rep, at):
    barrier = pltpu.get_barrier_semaphore()
    for axis in "yxz":
        for delta in (1, 2, 3):
            pl.semaphore_signal(
                barrier, inc=1, device_id=(shifted(dom, at, axis, delta), rep), device_id_type=MESH
            )
    pl.semaphore_signal(barrier, inc=1, device_id=(dom, 1 - rep), device_id_type=MESH)


class Copies:
    def __init__(self, send, recv):
        self.send, self.recv, self.used, self.open = send, recv, 0, []

    def take(self):
        self.used += 1
        return self.used - 1

    def start(self, number, src, dst, device):
        copy = pltpu.make_async_remote_copy(
            src_ref=src,
            dst_ref=dst,
            send_sem=self.send.at[number],
            recv_sem=self.recv.at[number],
            device_id=device,
            device_id_type=MESH,
        )
        copy.start()
        self.open.append(copy)

    def arrived(self, number, dst, device):
        pltpu.make_async_remote_copy(
            src_ref=dst,
            dst_ref=dst,
            send_sem=self.send.at[number],
            recv_sem=self.recv.at[number],
            device_id=device,
            device_id_type=MESH,
        ).wait_recv()

    def close(self):
        for copy in self.open:
            copy.wait_send()
        self.open = []


def one_hot(picks, counts, rows, base):
    nodes = picks[0].shape[1]
    row = lax.broadcasted_iota(jnp.int16, (rows, nodes), 0)
    table = jnp.zeros((rows, nodes), jnp.bfloat16)
    for pick, count in zip(picks, counts):
        here = jnp.broadcast_to(pick - base, (rows, nodes)).astype(jnp.int16)
        table = jnp.where(
            here == row, jnp.broadcast_to(count.astype(jnp.bfloat16), (rows, nodes)), table
        )
    return table


def ones_at(pick, rows, base=0):
    row = lax.broadcasted_iota(jnp.int32, (rows, pick.shape[1]), 0)
    return jnp.where(pick - base == row, 1.0, 0.0).astype(jnp.bfloat16)


def dot(a, b, over_a=1, over_b=0):
    return lax.dot_general(
        a, b, (((over_a,), (over_b,)), ((), ())), preferred_element_type=jnp.float32
    )


def side_by_side(rep, own, other, axis):
    first = jnp.where(rep == 0, own, other)
    second = jnp.where(rep == 0, other, own)
    return jnp.concatenate([first, second], axis=axis)


NORM = 131072.0**-0.5
N_COPIES = 420
PIECES = (0, 3, 1, 2)
ORDER = (2, 1, 3, 0)
BF, F32, I32 = jnp.bfloat16, jnp.float32, jnp.int32
SCRATCH = (
    [("g%d" % c, (4, 4, 4, UNIT, 128), BF) for c in range(3)]
    + [("x0", (4, 4, 2, UNIT, 128), BF), ("x1", (2, 4, 4, UNIT, 128), BF), ("x2", (4, 2, 4, UNIT, 128), BF)]
    + [("give0", (4, 4, 2, SHARE[0], 128), BF), ("give1", (2, 4, 4, SHARE[1], 128), BF)]
    + [("give2", (4, 2, 4, SHARE[2], 128), BF)]
    + [(name, (4, 4, 4, 1, 128), I32) for name in ("l1", "l2", "l3")]
    + [("featx", (1024, 128), BF), ("cotx", (1024, 128), BF), ("wsx", (128, 256), BF), ("wnx", (128, 256), BF)]
    + [("chooser", (2048, 288), BF), ("units", (288, 128), BF)]
    + [("picks", (16, 2048), I32), ("mult", (16, 2048), F32), ("table", (6144, 256), BF)]
    + [("total", (2048, 256), F32), ("totalx", (1024, 256), F32), ("grad", (2048, 256), BF)]
    + [("agg_send", (1024, 128), BF), ("out_send", (1024, 128), BF), ("agg_cols", (2048, 128), BF)]
    + [("terms", (4, 4, 4, 8, 128), F32), ("sums", (4, 4, 4, 8, 128), F32)]
    + [("local_sums", (2048, 256), BF)]
    + [("w1", (3, 4, 4, 8, 128), F32), ("w2", (3, 4, 8, 128), F32), ("wb", (4, 4, 8, 128), F32)]
    + [("wc", (4, 8, 128), F32), ("w3", (3, 8, 128), F32)]
    + [("r%d" % c, (2, SHARE[c], 128), F32) for c in range(3)]
    + [("whole%d" % c, (4, 4, 4, SHARE[c], 128), BF) for c in range(3)]
    + [("first%d" % c, (4, 4, SHARE[c], 128), BF) for c in range(3)]
    + [("second%d" % c, (4, SHARE[c], 128), BF) for c in range(3)]
    + [("inner%d" % c, (3, SHARE[c], 128), BF) for c in range(3)]
    + [
        ("%s%d%d" % (stage, c, n), lead + (2 if n < 2 else 4, SHARE[c], 128), BF)
        for stage, lead in (("outer", (4,)), ("middle", ()))
        for c in range(3)
        for n in range(4)
    ]
)


def layer_kernel(*refs):
    features, cotangent, self_weight, neighbor_weight, local_in, halo_in, hub_in = refs[:7]
    brows, hrows, lists, counts = refs[7:11]
    output, gradient, grad_self, grad_neighbor = refs[11:15]
    named = {name: ref for (name, _, _), ref in zip(SCRATCH, refs[15:])}
    send, recv, local = refs[15 + len(SCRATCH) :]
    g0, g1, g2 = bufs = [named["g%d" % c] for c in range(3)]
    x0, x1, x2 = [named["x%d" % c] for c in range(3)]
    give0, give1, give2 = [named["give%d" % c] for c in range(3)]
    l1, l2, l3 = named["l1"], named["l2"], named["l3"]
    featx, cotx, wsx, wnx = named["featx"], named["cotx"], named["wsx"], named["wnx"]
    chooser, units, picks, mult = named["chooser"], named["units"], named["picks"], named["mult"]
    table, total, totalx, grad = named["table"], named["total"], named["totalx"], named["grad"]
    agg_send, out_send, agg_cols = named["agg_send"], named["out_send"], named["agg_cols"]
    terms, sums, local_sums = named["terms"], named["sums"], named["local_sums"]
    w1, w2, wb, wc, w3 = (named[name] for name in ("w1", "w2", "wb", "wc", "w3"))
    results = [named["r%d" % c] for c in range(3)]
    wholes = [named["whole%d" % c] for c in range(3)]
    firsts = [named["first%d" % c] for c in range(3)]
    seconds = [named["second%d" % c] for c in range(3)]
    outer_recv, middle_recv = (
        [[named["%s%d%d" % (stage, c, n)] for n in range(4)] for c in range(3)]
        for stage in ("outer", "middle")
    )
    inner_recv = [named["inner%d" % c] for c in range(3)]
    dom, rep, at = place()
    other = (dom, 1 - rep)
    io = Copies(send, recv)
    signal_all(dom, rep, at)
    chooser[:, 0:256] = ones_at(brows[...], 2048)
    chooser[:, 256:288] = ones_at(hrows[...], 2048)
    units[...] = dot(chooser[...], features[...], 0, 0).astype(BF)
    pl.semaphore_wait(pltpu.get_barrier_semaphore(), 10)

    def prepare():
        halo = halo_in[...]
        end = jnp.int32(0)
        sender = jnp.zeros_like(halo)
        before = jnp.zeros_like(halo)
        for p in range(64):
            end = end + counts[0, p]
            passed = halo >= end
            sender = sender + jnp.where(passed, 1, 0)
            before = before + jnp.where(passed, counts[0, p], 0)
        sender = jnp.minimum(sender, 63)
        slot = jnp.clip(halo - before, 0, 127)

        def in_half(p, within, size):
            number = (p >> 2) * 2 + (p & 1)
            return jnp.where(((p & 3) >> 1) == rep, number * size + within, -1)

        hub = hub_in[...]
        local = local_in[...] - rep * 1024
        local = jnp.where((local >= 0) & (local < 1024), local, -1)
        groups = (local, in_half(sender, slot, 128), in_half(hub >> 5, hub & 31, 32))
        start = 0
        for group in groups:
            size = group.shape[0]
            picks[start : start + size] = group
            for a in range(size):
                total = jnp.zeros((1, group.shape[1]), jnp.float32)
                for b in range(size):
                    total = total + jnp.where(group[a : a + 1] == group[b : b + 1], 1.0, 0.0)
                mult[start + a : start + a + 1] = total
            start += size

    def local_gather(tile):
        cols = slice(tile * 512, tile * 512 + 512)
        chosen = [picks[k : k + 1, cols] for k in range(8)]
        counts_of = [mult[k : k + 1, cols] for k in range(8)]
        total[cols] = dot(one_hot(chosen, counts_of, 512, 0), table[0:512], 0, 0) + dot(
            one_hot(chosen, counts_of, 512, 512), table[512:1024], 0, 0
        )

    coords = [tuple(at[a] for a in CHAINS[chain]) for chain in range(3)]
    ways = [
        [
            ((shifted(dom, at, a, 1), rep), (shifted(dom, at, a, 3), rep))
            for a in CHAINS[chain]
        ]
        for chain in range(3)
    ]

    inner_ids = [[io.take() for _ in range(3)] for _ in range(3)]
    mine = []
    for chain in range(3):
        o, m, i = coords[chain]
        unit = units.at[pl.ds(chain * UNIT, UNIT)]
        for delta in (1, 3, 2):
            device = (shifted(dom, at, CHAINS[chain][2], delta), rep)
            io.start(inner_ids[chain][delta - 1], unit, bufs[chain].at[o, m, i], device)
        copy = pltpu.make_async_copy(unit, bufs[chain].at[o, m, i], local.at[chain])
        copy.start()
        mine.append(copy)

    list_steps = (
        ("y", lambda j: lists.at[j], lambda j: l1.at[j]),
        ("x", lambda j: l1.at[:, j], lambda j: l2.at[j]),
        ("z", lambda j: l2.at[:, :, j], lambda j: l3.at[j]),
    )
    list_ids = [[io.take() for _ in range(3)] for _ in range(3)]

    def send_lists(step):
        axis, src, dst = list_steps[step]
        for delta in (1, 2, 3):
            there = (at[axis] + delta) % 4
            io.start(
                list_ids[step][delta - 1],
                src(there),
                dst(at[axis]),
                (shifted(dom, at, axis, delta), rep),
            )
        copy = pltpu.make_async_copy(src(at[axis]), dst(at[axis]), local.at[3])
        copy.start()
        return copy

    def take_lists(step, copy):
        axis, _, dst = list_steps[step]
        copy.wait()
        for delta in (1, 2, 3):
            io.arrived(list_ids[step][delta - 1], dst((at[axis] - delta) % 4), other)

    theirs = pl.ds(pl.multiple_of((1 - rep) * 1024, 1024), 1024)
    pairs = (
        (features.at[theirs], featx),
        (self_weight, wsx),
        (neighbor_weight, wnx),
        (cotangent.at[theirs], cotx),
    )
    pair_ids = [io.take() for _ in pairs]
    for number, (src, dst) in zip(pair_ids, pairs):
        io.start(number, src, dst, other)
    listed = send_lists(0)

    swap0, swap1, swap2 = io.used, io.used + 16, io.used + 24
    io.used += 32

    def swap(chain, o, m):
        if chain == 0:
            pltpu.make_async_remote_copy(
                src_ref=g0.at[o, m, pl.ds(2 * (1 - rep), 2)],
                dst_ref=x0.at[o, m],
                send_sem=send.at[swap0 + o * 4 + m],
                recv_sem=recv.at[swap0 + o * 4 + m],
                device_id=other,
                device_id_type=MESH,
            ).start()
            return
        z = o if chain == 1 else m

        @pl.when(z // 2 != rep)
        def _():
            if chain == 1:
                number, dst = swap1 + (o % 2) * 4 + m, x1.at[o % 2, m]
            else:
                number, dst = swap2 + o * 2 + m % 2, x2.at[o, m % 2]
            pltpu.make_async_remote_copy(
                src_ref=bufs[chain].at[o, m],
                dst_ref=dst,
                send_sem=send.at[number],
                recv_sem=recv.at[number],
                device_id=other,
                device_id_type=MESH,
            ).start()

    middle_ids = [[io.take() for _ in range(4)] for _ in range(3)]
    outer_ids = [[[io.take() for _ in range(4)] for _ in range(4)] for _ in range(3)]

    def spread(chain, piece):
        o, m, _ = coords[chain]
        up, down = ways[chain][0]
        block = bufs[chain].at[o, (m + piece) % 4]
        ids = outer_ids[chain][piece]
        io.start(ids[0], block, block, up)
        io.start(ids[1], block, block, down)
        swap(chain, o, (m + piece) % 4)

    def pass_on(chain, ids, from_down, from_up, half, up, down):
        io.arrived(ids[0], from_down, down)
        io.start(ids[2], half(from_down, 0), half(from_down, 0), up)
        io.arrived(ids[1], from_up, up)
        io.start(ids[3], half(from_up, 1), half(from_up, 1), down)

    def units_half(ref, which):
        return ref.at[pl.ds(which * 2, 2)]


    def inner_end():
        for chain in range(3):
            o, m, i = coords[chain]
            mine[chain].wait()
            for delta in (1, 3, 2):
                io.arrived(inner_ids[chain][delta - 1], bufs[chain].at[o, m, (i - delta) % 4], other)
            up, down = ways[chain][1]
            block = bufs[chain].at[o, m]
            io.start(middle_ids[chain][0], block, block, up)
            io.start(middle_ids[chain][1], block, block, down)
            spread(chain, 0)

    def middle_pass():
        for chain in range(3):
            o, m, i = coords[chain]
            up, down = ways[chain][1]
            buf = bufs[chain]
            pass_on(
                chain,
                middle_ids[chain],
                buf.at[o, (m + 3) % 4],
                buf.at[o, (m + 1) % 4],
                units_half,
                up,
                down,
            )
            spread(chain, 3)
            spread(chain, 1)

    def middle_end():
        for chain in range(3):
            o, m, i = coords[chain]
            up, down = ways[chain][1]
            far = bufs[chain].at[o, (m + 2) % 4]
            io.arrived(middle_ids[chain][2], units_half(far, 0), down)
            io.arrived(middle_ids[chain][3], units_half(far, 1), up)
            spread(chain, 2)

    def spread_pass(piece):
        for chain in range(3):
            o, m, i = coords[chain]
            up, down = ways[chain][0]
            buf, at_m = bufs[chain], (m + piece) % 4
            pass_on(
                chain,
                outer_ids[chain][piece],
                buf.at[(o + 3) % 4, at_m],
                buf.at[(o + 1) % 4, at_m],
                units_half,
                up,
                down,
            )
            swap(chain, (o + 3) % 4, at_m)
            swap(chain, (o + 1) % 4, at_m)

    def spread_end(piece):
        for chain in range(3):
            o, m, i = coords[chain]
            up, down = ways[chain][0]
            far = bufs[chain].at[(o + 2) % 4, (m + piece) % 4]
            io.arrived(outer_ids[chain][piece][2], units_half(far, 0), down)
            io.arrived(outer_ids[chain][piece][3], units_half(far, 1), up)
            swap(chain, (o + 2) % 4, (m + piece) % 4)

    inner_end()
    prepare()
    take_lists(0, listed)
    listed = send_lists(1)
    for number, (_, dst) in zip(pair_ids, pairs):
        io.arrived(number, dst, other)
    own_rows = pl.ds(pl.multiple_of(rep * 1024, 1024), 1024)
    table[0:1024] = side_by_side(rep, features[own_rows], featx[...], 1)
    middle_pass()
    take_lists(1, listed)
    listed = send_lists(2)
    spread_pass(0)
    middle_end()
    local_gather(0)
    spread_end(0)
    spread_pass(3)
    local_gather(1)
    spread_pass(1)
    local_gather(2)
    spread_end(3)
    spread_pass(2)
    local_gather(3)
    take_lists(2, listed)
    spread_end(1)
    spread_end(2)

    def settle(number, ref):
        copy = pltpu.make_async_remote_copy(
            src_ref=ref,
            dst_ref=ref,
            send_sem=send.at[number],
            recv_sem=recv.at[number],
            device_id=other,
            device_id_type=MESH,
        )
        copy.wait_recv()
        copy.wait_send()

    for a in range(4):
        for b in range(4):
            settle(swap0 + a * 4 + b, x0.at[a, b])
        for b in range(2):
            settle(swap1 + b * 4 + a, x1.at[b, a])
            settle(swap2 + a * 2 + b, x2.at[a, b])

    def select(number, carry):
        y, x, z = number // 8, (number // 2) % 4, number % 2
        zz = 2 * rep + z
        wide = [
            side_by_side(rep, own, came, 1)
            for own, came in (
                (g0[y, x, zz], x0[y, x, z]),
                (g1[zz, y, x], x1[z, y, x]),
                (g2[x, zz, y], x2[x, z, y]),
            )
        ]
        rows = jnp.concatenate([wide[0], wide[1], wide[2][:64]], axis=0)
        slots = dot(ones_at(l3[zz, x, y], 256), rows, 0, 0)
        table[pl.ds(pl.multiple_of(1024 + number * 128, 128), 128)] = slots.astype(jnp.bfloat16)
        table[pl.ds(pl.multiple_of(5120 + number * 32, 32), 32)] = wide[2][64:]
        return carry

    lax.fori_loop(0, 32, select, 0, unroll=32)

    def gather_tile(tile):
        cols = pl.ds(pl.multiple_of(tile * 512, 512), 512)
        value = total[cols]
        for first, some, begin, end in ((8, 4, 1024, 5120), (12, 4, 5120, 6144)):
            chosen = [picks[k : k + 1, cols] for k in range(first, first + some)]
            counts_of = [mult[k : k + 1, cols] for k in range(first, first + some)]
            for base in range(begin, end, 512):
                value = value + dot(
                    one_hot(chosen, counts_of, 512, base - begin), table[base : base + 512], 0, 0
                )
        total[cols] = value

    sums_at = io.used
    io.used += 2

    def sum_copy(k, tile):
        cols = pl.ds(pl.multiple_of(tile * 512, 512), 512)
        return pltpu.make_async_remote_copy(
            src_ref=total.at[cols],
            dst_ref=totalx.at[pl.ds(pl.multiple_of(k * 512, 512), 512)],
            send_sem=send.at[sums_at + k],
            recv_sem=recv.at[sums_at + k],
            device_id=other,
            device_id_type=MESH,
        )

    def gather_theirs(k, carry):
        gather_tile((1 - rep) * 2 + k)
        sum_copy(k, (1 - rep) * 2 + k).start()
        return carry

    def gather_mine(k, carry):
        gather_tile(rep * 2 + k)
        return carry

    lax.fori_loop(0, 2, gather_theirs, 0)
    lax.fori_loop(0, 2, gather_mine, 0)

    selfw = side_by_side(rep, self_weight[...], wsx[...], 0)
    nbrw = side_by_side(rep, neighbor_weight[...], wnx[...], 0)
    grad_ids = [[io.take() for _ in range(3)] for _ in range(2)]
    for step in range(4):
        if step % 2 == 0:
            sum_copy(step // 2, (1 - rep) * 2 + step // 2).wait_recv()
        rows = pl.ds(pl.multiple_of(rep * 1024 + step * 256, 256), 256)
        part = slice(step * 256, step * 256 + 256)
        wide = side_by_side(rep, features[rows], featx[part], 1)
        cotan = side_by_side(rep, cotangent[rows], cotx[part], 1)
        aggregate = ((total[rows] + totalx[part]) * (1.0 / 16.0)).astype(jnp.bfloat16)
        pre_act = dot(wide, selfw) + dot(aggregate, nbrw)
        sigmoid = 1.0 / (1.0 + jnp.exp(-pre_act))
        result = (pre_act * sigmoid).astype(jnp.bfloat16)
        slope = sigmoid * (1.0 + pre_act * (1.0 - sigmoid))
        grad[rows] = (cotan.astype(jnp.float32) * slope).astype(jnp.bfloat16)
        agg_send[part] = jnp.where(rep == 0, aggregate[:, 128:], aggregate[:, :128])
        out_send[part] = jnp.where(rep == 0, result[:, 128:], result[:, :128])
        agg_cols[rows] = jnp.where(rep == 0, aggregate[:, :128], aggregate[:, 128:])
        output[rows] = jnp.where(rep == 0, result[:, :128], result[:, 128:])
        if step % 2 == 1:
            n = grad_ids[step // 2]
            tall = pl.ds(pl.multiple_of(rep * 1024 + (step // 2) * 512, 512), 512)
            flat = pl.ds((step // 2) * 512, 512)
            io.start(n[0], grad.at[tall], grad.at[tall], other)
            io.start(n[1], agg_send.at[flat], agg_cols.at[tall], other)
            io.start(n[2], out_send.at[flat], output.at[tall], other)
    for k in range(2):
        sum_copy(k, (1 - rep) * 2 + k).wait_send()

    own_terms = (
        dot(features[own_rows], grad[own_rows], 0, 0),
        dot(agg_cols[own_rows], grad[own_rows], 0, 0),
    )
    for k in range(2):
        tall = pl.ds(pl.multiple_of((1 - rep) * 1024 + k * 512, 512), 512)
        io.arrived(grad_ids[k][0], grad.at[tall], other)
        io.arrived(grad_ids[k][1], agg_cols.at[tall], other)

    def finish_terms():
        for n, (mine_term, data) in enumerate(zip(own_terms, (features, agg_cols))):
            term = mine_term + dot(data[theirs], grad[theirs], 0, 0)
            for h in range(2):
                for b in range(16):
                    terms[2 * n + h, b // 4, b % 4] = term[b * 8 : b * 8 + 8, h * 128 : h * 128 + 128]

    def scatter_step(step, carry):
        sums_of = jnp.zeros((640, 256), jnp.float32)
        for begin in range(0, 2048, 256):
            cols = slice(begin, begin + 256)
            parts = []
            for first, some, rows in ((8, 4, 512), (12, 4, 128)):
                chosen = [picks[k : k + 1, cols] for k in range(first, first + some)]
                counts_of = [mult[k : k + 1, cols] for k in range(first, first + some)]
                parts.append(one_hot(chosen, counts_of, rows, step * rows))
            sums_of = sums_of + dot(jnp.concatenate(parts, axis=0), grad[cols])
        slots = sums_of[0:512].astype(jnp.bfloat16)
        hubs = sums_of[512:640].astype(jnp.bfloat16)
        for k in range(4):
            y, x, z = step // 2, (step % 2) * 2 + k // 2, k % 2
            zz = 2 * rep + z
            rows = dot(ones_at(l3[zz, x, y], 256), slots[k * 128 : k * 128 + 128])
            rows = rows.astype(jnp.bfloat16)
            rows = jnp.concatenate([rows, hubs[k * 32 : k * 32 + 32]], axis=0)
            keep = jnp.where(rep == 0, rows[:, :128], rows[:, 128:])
            give = jnp.where(rep == 0, rows[:, 128:], rows[:, :128])
            parts = [slice(a, a + n) for a, n in zip(SHARE_AT, SHARE)]
            wholes[0][y, x, zz], give0[y, x, z] = keep[parts[0]], give[parts[0]]
            wholes[1][zz, y, x], give1[z, y, x] = keep[parts[1]], give[parts[1]]
            wholes[2][x, zz, y], give2[x, z, y] = keep[parts[2]], give[parts[2]]
        return carry

    def output_done():
        for k in range(2):
            tall = pl.ds(pl.multiple_of((1 - rep) * 1024 + k * 512, 512), 512)
            io.arrived(grad_ids[k][2], output.at[tall], other)

    def trade(axis, src, dst):
        ids = [io.take() for _ in range(3)]
        for delta in (1, 2, 3):
            device = (shifted(dom, at, axis, delta), rep)
            io.start(ids[delta - 1], src(delta), dst(delta), device)
        return ids

    def traded(ids, dst):
        for delta in (1, 2, 3):
            io.arrived(ids[delta - 1], dst(delta), other)

    def reduce_start(axis, src, landing):
        return trade(axis, lambda d: src.at[(at[axis] + d) % 4], lambda d: landing.at[d - 1])

    def reduce_end(ids, src, axis, landing):
        traded(ids, lambda d: landing.at[d - 1])
        return src[at[axis]] + landing[0] + landing[1] + landing[2]

    def give_start(axis, ref):
        return trade(axis, lambda d: ref(at[axis]), lambda d: ref(at[axis]))

    def give_end(ids, axis, ref):
        traded(ids, lambda d: ref((at[axis] - d) % 4))

    gives = {
        "z": lambda j: sums.at[at["y"], at["x"], j],
        "x": lambda j: sums.at[at["y"], j],
        "y": lambda j: sums.at[j],
    }

    swap_ids = [[io.take() for _ in range(4)] for _ in range(3)]

    def swap_refs(chain, piece, half):
        m = (coords[chain][1] + piece) % 4
        span = pl.ds(2 * half, 2)
        if chain == 0:
            return give0.at[:, m], wholes[0].at[:, m, span]
        if chain == 1:
            return give1.at[:, m], wholes[1].at[span, m]
        return give2.at[:, m % 2], wholes[2].at[:, m]

    def remote(number, src, dst):
        return pltpu.make_async_remote_copy(
            src_ref=src,
            dst_ref=dst,
            send_sem=send.at[number],
            recv_sem=recv.at[number],
            device_id=other,
            device_id_type=MESH,
        )

    def swap_start(chain, piece):
        number = swap_ids[chain][piece]
        src, dst = swap_refs(chain, piece, rep)

        def go():
            remote(number, src, dst).start()

        if chain == 2:
            pl.when((coords[2][1] + piece) % 4 // 2 == rep)(go)
        else:
            go()

    def swap_end(chain, piece):
        number = swap_ids[chain][piece]
        src, dst = swap_refs(chain, piece, rep)
        _, came = swap_refs(chain, piece, 1 - rep)

        def kept():
            remote(number, src, dst).wait_send()

        def got():
            remote(number, came, came).wait_recv()

        if chain == 2:
            here = (coords[2][1] + piece) % 4 // 2 == rep
            pl.when(here)(kept)
            pl.when(jnp.logical_not(here))(got)
        else:
            kept()
            got()


    outer_ids = [[[io.take() for _ in range(6)] for _ in range(4)] for _ in range(3)]
    middle_ids = [[io.take() for _ in range(6)] for _ in range(3)]
    inner_ids = [[io.take() for _ in range(3)] for _ in range(3)]
    low2, high2 = pl.ds(0, 2), pl.ds(2, 2)

    def add_into(spot, came):
        spot[...] = (spot[...].astype(jnp.float32) + came[...].astype(jnp.float32)).astype(jnp.bfloat16)

    def three(a, b, c):
        return a[...].astype(jnp.float32) + b[...].astype(jnp.float32) + c[...].astype(jnp.float32)

    def outer_start(piece, chains):
        for chain in chains:
            swap_end(chain, piece)
            o, m, i = coords[chain]
            up, down = ways[chain][0]
            data, m = wholes[chain], (m + piece) % 4
            from_low, from_high, whole_low, whole_high = (r.at[piece] for r in outer_recv[chain])
            n = outer_ids[chain][piece]
            io.start(n[0], data.at[(o + 2) % 4, m, low2], from_low, up)
            io.start(n[1], data.at[(o + 2) % 4, m, high2], from_high, down)
            io.start(n[2], data.at[(o + 1) % 4, m, high2], whole_low.at[high2], up)
            io.start(n[3], data.at[(o + 3) % 4, m, low2], whole_high.at[low2], down)

    def outer_pass(piece, chains):
        for chain in chains:
            o, m, i = coords[chain]
            up, down = ways[chain][0]
            data, m = wholes[chain], (m + piece) % 4
            from_low, from_high, whole_low, whole_high = (r.at[piece] for r in outer_recv[chain])
            n = outer_ids[chain][piece]
            io.arrived(n[0], from_low, other)
            for k in range(2):
                add_into(data.at[(o + 1) % 4, m, k], from_low.at[k])
            io.start(n[4], data.at[(o + 1) % 4, m, low2], whole_low.at[low2], up)
            io.arrived(n[1], from_high, other)
            for k in range(2):
                add_into(data.at[(o + 3) % 4, m, 2 + k], from_high.at[k])
            io.start(n[5], data.at[(o + 3) % 4, m, high2], whole_high.at[high2], down)

    def outer_end(piece, chains):
        for chain in chains:
            o, m, i = coords[chain]
            data, target = wholes[chain], firsts[chain].at[piece]
            _, _, whole_low, whole_high = (r.at[piece] for r in outer_recv[chain])
            n = outer_ids[chain][piece]
            io.arrived(n[2], whole_low.at[high2], other)
            io.arrived(n[3], whole_high.at[low2], other)
            io.arrived(n[4], whole_low.at[low2], other)
            io.arrived(n[5], whole_high.at[high2], other)
            for k in range(4):
                target[k] = three(
                    data.at[o, (m + piece) % 4, k], whole_low.at[k], whole_high.at[k]
                ).astype(jnp.bfloat16)
            up, down = ways[chain][1]
            from_low, from_high, whole_low, whole_high = middle_recv[chain]
            n = middle_ids[chain]
            if piece == 2:
                io.start(n[0], target.at[low2], from_low, up)
                io.start(n[1], target.at[high2], from_high, down)
            if piece == 1:
                io.start(n[2], target.at[high2], whole_low.at[high2], up)
            if piece == 3:
                io.start(n[3], target.at[low2], whole_high.at[low2], down)


    local_ids = [io.take() for _ in range(4)]

    def local_scatter(part):
        value = jnp.zeros((256, 256), jnp.float32)
        for begin in range(0, 2048, 512):
            cols = slice(begin, begin + 512)
            chosen = [picks[k : k + 1, cols] for k in range(8)]
            counts_of = [mult[k : k + 1, cols] for k in range(8)]
            value = value + dot(one_hot(chosen, counts_of, 256, part * 256), grad[cols])
        rows = pl.ds(pl.multiple_of(rep * 1024 + part * 256, 256), 256)
        local_sums[rows] = (value * (1.0 / 16.0)).astype(jnp.bfloat16)
        io.start(local_ids[part], local_sums.at[rows], local_sums.at[rows], other)

    def products(half):
        if half == 0:
            for part in range(4):
                rows = pl.ds(pl.multiple_of((1 - rep) * 1024 + part * 256, 256), 256)
                io.arrived(local_ids[part], local_sums.at[rows], other)
        for begin in range(half * 1024, half * 1024 + 1024, 512):
            rows = slice(begin, begin + 512)
            total[rows, 0:128] = dot(grad[rows], self_weight[...], 1, 1) + dot(
                local_sums[rows], neighbor_weight[...], 1, 1
            )

    def reduce_pass(chains):
        for chain in chains:
            up, down = ways[chain][1]
            from_low, from_high, whole_low, whole_high = middle_recv[chain]
            n = middle_ids[chain]
            io.arrived(n[0], from_low, other)
            for k in range(2):
                add_into(firsts[chain].at[1, k], from_low.at[k])
            io.start(n[4], firsts[chain].at[1, low2], whole_low.at[low2], up)
            io.arrived(n[1], from_high, other)
            for k in range(2):
                add_into(firsts[chain].at[3, 2 + k], from_high.at[k])
            io.start(n[5], firsts[chain].at[3, high2], whole_high.at[high2], down)

    def reduce_last(chains):
        for chain in chains:
            o, m, i = coords[chain]
            from_low, from_high, whole_low, whole_high = middle_recv[chain]
            n = middle_ids[chain]
            io.arrived(n[2], whole_low.at[high2], other)
            io.arrived(n[3], whole_high.at[low2], other)
            io.arrived(n[4], whole_low.at[low2], other)
            io.arrived(n[5], whole_high.at[high2], other)
            target = seconds[chain]
            for k in range(4):
                target[k] = three(
                    firsts[chain].at[0, k], whole_low.at[k], whole_high.at[k]
                ).astype(jnp.bfloat16)
            for delta in (2, 1, 3):
                device = (shifted(dom, at, CHAINS[chain][2], delta), rep)
                io.start(
                    inner_ids[chain][delta - 1],
                    target.at[(i + delta) % 4],
                    inner_recv[chain].at[delta - 1],
                    device,
                )

    def scatter_piece(piece):
        first = 2 * ((at["y"] + piece) % 4)
        lax.fori_loop(0, 2, lambda k, carry: scatter_step(first + k, carry), 0)

    early, late = (1,), (0, 2)
    scatter_piece(2)
    swap_start(1, 2)
    scatter_piece(1)
    swap_start(1, 1)
    outer_start(2, early)
    scatter_piece(3)
    swap_start(1, 3)
    outer_start(1, early)
    outer_pass(2, early)
    scatter_piece(0)
    for piece in (2, 1):
        for chain in late:
            swap_start(chain, piece)
    swap_start(1, 0)
    for piece in (3, 0):
        for chain in late:
            swap_start(chain, piece)
    finish_terms()
    weigh = reduce_start("y", terms, w1)
    outer_start(3, early)
    outer_pass(1, early)
    outer_end(2, early)
    outer_start(2, late)
    local_scatter(0)
    wb[...] = reduce_end(weigh, terms, "y", w1)
    weigh = reduce_start("x", wb, w2)
    outer_pass(3, early)
    outer_start(1, late)
    outer_end(1, early)
    outer_pass(2, late)
    outer_start(0, early)
    outer_start(3, late)
    wc[...] = reduce_end(weigh, wb, "x", w2)
    weigh = reduce_start("z", wc, w3)
    outer_end(3, early)
    local_scatter(1)
    outer_pass(1, late)
    outer_end(2, late)
    sums[at["y"], at["x"], at["z"]] = reduce_end(weigh, wc, "z", w3)
    weigh = give_start("z", gives["z"])
    outer_pass(0, early)
    reduce_pass(early)
    outer_start(0, late)
    local_scatter(2)
    outer_pass(3, late)
    outer_end(1, late)
    give_end(weigh, "z", gives["z"])
    weigh = give_start("x", gives["x"])
    outer_end(0, early)
    reduce_last(early)
    outer_pass(0, late)
    local_scatter(3)
    outer_end(3, late)
    reduce_pass(late)
    outer_end(0, late)
    reduce_last(late)
    give_end(weigh, "x", gives["x"])
    weigh = give_start("y", gives["y"])
    products(0)
    products(1)
    last = [io.take() for _ in range(3)]
    for chain in (1, 0, 2):
        o, m, i = coords[chain]
        came = inner_recv[chain]
        for delta in (1, 3, 2):
            io.arrived(inner_ids[chain][delta - 1], came.at[delta - 1], other)
        results[chain][rep] = three(seconds[chain].at[i], came.at[0], came.at[2]) + came[1].astype(
            jnp.float32
        )
        io.start(last[chain], results[chain].at[rep], results[chain].at[rep], other)
    give_end(weigh, "y", gives["y"])
    for n, target in enumerate((grad_self, grad_neighbor)):
        for h in range(2):
            for b in range(16):
                target[b * 8 : b * 8 + 8, h * 128 : h * 128 + 128] = (
                    sums[2 * n + h, b // 4, b % 4] * NORM
                )
    for chain in range(3):
        io.arrived(last[chain], results[chain].at[1 - rep], other)
    output_done()
    tall = jnp.concatenate(
        [jnp.concatenate([r[0], r[1]], axis=1) for r in results], axis=0
    )
    value = dot((tall * (1.0 / 16.0)).astype(jnp.bfloat16), neighbor_weight[...], 1, 1)
    high = value.astype(jnp.bfloat16)
    low = (value - high.astype(jnp.float32)).astype(jnp.bfloat16)
    pieces = jnp.concatenate([high, low], axis=1)
    for begin in range(0, 2048, 512):
        rows = slice(begin, begin + 512)
        both = dot(chooser[rows], pieces)
        gradient[rows] = (
            total[rows, 0:128] + both[:, 0:128] + both[:, 128:256]
        ).astype(jnp.bfloat16)
    io.close()


def layer_call(*args):
    return pl.pallas_call(
        layer_kernel,
        out_shape=[jax.ShapeDtypeStruct((2048, 128), BF)] * 2
        + [jax.ShapeDtypeStruct((128, 256), F32)] * 2,
        in_specs=[VMEM_SPEC] * 10 + [pl.BlockSpec(memory_space=pltpu.SMEM)],
        out_specs=[VMEM_SPEC] * 4,
        scratch_shapes=[pltpu.VMEM(shape, kind) for _, shape, kind in SCRATCH]
        + [
            pltpu.SemaphoreType.DMA((N_COPIES,)),
            pltpu.SemaphoreType.DMA((N_COPIES,)),
            pltpu.SemaphoreType.DMA((4,)),
        ],
        compiler_params=pltpu.CompilerParams(
            collective_id=0, has_side_effects=True, vmem_limit_bytes=BIG
        ),
        name="layer",
    )(*args)


def hand_over_kernel(*refs):
    for source, target in zip(refs[:4], refs[4:]):
        target[...] = source[...]


def hand_over(*arrays):
    return pl.pallas_call(
        hand_over_kernel,
        out_shape=[jax.ShapeDtypeStruct(a.shape, a.dtype) for a in arrays],
        in_specs=[VMEM_SPEC] * 4,
        out_specs=[VMEM_SPEC] * 4,
        name="hand_over",
    )(*arrays)


def per_device(
    features,
    cotangent,
    self_weight,
    neighbor_weight,
    local_neighbors,
    hub_rows,
    hub_neighbors,
    boundary_rows,
    send_lists,
    received_counts,
    halo_neighbors,
):
    output, gradient, grad_self, grad_neighbor = layer_call(
        features,
        cotangent,
        self_weight,
        neighbor_weight,
        local_neighbors.T,
        halo_neighbors.T,
        hub_neighbors.T,
        boundary_rows[None],
        hub_rows[None],
        send_lists.reshape(4, 4, 4, 1, 128),
        received_counts,
    )
    return tuple(hand_over(output, gradient, grad_self, grad_neighbor))


def solution(mesh):
    return jax.shard_map(
        per_device,
        mesh=mesh,
        in_specs=(
            P("dom", "rep"),
            P("dom", "rep"),
            P("rep", None),
            P("rep", None),
            P("dom", None),
            P("dom"),
            P("dom", None),
            P("dom"),
            P("dom", None, None),
            P("dom", None),
            P("dom", None),
        ),
        out_specs=(P("dom", "rep"), P("dom", "rep"), P("rep", None), P("rep", None)),
        check_vma=False,
    )
```
